256 devices in a mesh: row: 8 (over z_lo, y), col: 32 (over z_hi, x, core).
Axes of the slice: x: 4, y: 4, z: 8 (z_hi: 4, z_lo: 2; z = z_hi * 2 + z_lo), core: 2. Of those that a mesh axis runs over, the one named last changes fastest.
Arguments:
- image: bfloat16 [128, 768, 768], P('row', 'col'), may hold values from -6 to 6
- conv_weight: float32 [7, 7, 768], replicated, may hold values from -0.875 to 0.875
- conv_bias: float32 [768], replicated, may hold values from -3 to 3
- layernorm_gain: float32 [768], replicated, may hold values from 0.5 to 1.5
- layernorm_bias: float32 [768], replicated, may hold values from -2 to 2
- w_expand: bfloat16 [3072, 768], replicated, may hold values from -0.21875 to 0.21875
- b_expand: float32 [3072], replicated, may hold values from -3 to 3
- w_reduce: bfloat16 [768, 3072], replicated, may hold values from -0.109375 to 0.109375
- b_reduce: float32 [768], replicated, may hold values from -3 to 3
- layer_scale: float32 [768], replicated, may hold values from 0.2 to 1.5
- cotangent: bfloat16 [128, 768, 768], P('row', 'col'), may hold values from -6 to 6
Outputs:
- grad_image: float32 [128, 768, 768], P('row', 'col')
- grad_expand: float32 [3072, 768], P(('row', 'col'))
- grad_reduce: float32 [768, 3072], P(None, ('row', 'col'))
- grad_conv_weight: float32 [7, 7, 768], replicated
- grad_conv_bias: float32 [768], replicated
- grad_ln_gain: float32 [768], replicated
- grad_ln_bias: float32 [768], replicated
- grad_b_expand: float32 [3072], replicated
- grad_b_reduce: float32 [768], replicated
- grad_layer_scale: float32 [768], replicated
The draws below stay inside these ranges and needn't reach their ends.
All inputs are finite; a program needn't handle non-finite values.
Results may differ from the reference program's by a relative error of at most 0.0075.
Values may be sent and summed in bfloat16 or wider, within the bound.
No kernel may reach another device: no remote copies, remote signals or barrier semaphores. Data moves between devices by JAX's collectives and lax.ppermute only.
A program may use at most 128 MiB of HBM per device.

```python
import math
import jax
import jax.numpy as jnp
from jax import lax

C = 768
F = 3072
KS = 7
HEIGHT = 128
WIDTH = 768


def shard_levels(own_key, dims, shards, smallest, high):
    factor_of = 1.0
    for dim, shards_of in shards:
        draws = jax.random.uniform(jax.random.fold_in(jax.random.fold_in(own_key, 6), dim), (shards_of,), jnp.float32, smallest / len(shards), high / len(shards))
        factor_of = factor_of * jnp.repeat(jnp.exp(draws), dims[dim] // shards_of).reshape((-1,) + (1,) * (len(dims) - 1 - dim))
    return factor_of


def noise(key, extent, spread, reach, pieces=(), held_as=jnp.bfloat16):
    drawn = spread * jax.random.normal(key, extent, jnp.float32)
    if pieces:
        drawn = drawn * shard_levels(key, extent, pieces, -0.22, 0.18)
    return jnp.clip(drawn, -reach, reach).astype(held_as)


def setup_inputs(seed: int = 0) -> dict:
    streams_of = jax.random.split(jax.random.key(seed), 12)
    image = noise(streams_of[0], (HEIGHT, WIDTH, C), 1.0, 6.0, ((0, 8), (1, 32)))
    conv_weight = noise(streams_of[1], (KS, KS, C), (KS * KS) ** -0.5, 0.875, (), jnp.float32)
    conv_bias = noise(streams_of[2], (C,), 0.5, 3.0, (), jnp.float32)
    layernorm_gain = jnp.clip(jax.random.uniform(streams_of[3], (C,), jnp.float32, 0.5, 1.5), 0.5, 1.5)
    layernorm_bias = noise(streams_of[4], (C,), 0.3, 2.0, (), jnp.float32)
    w_expand = noise(streams_of[5], (F, C), C ** -0.5, 0.21875)
    b_expand = noise(streams_of[6], (F,), 0.5, 3.0, (), jnp.float32)
    w_reduce = noise(streams_of[7], (C, F), F ** -0.5, 0.109375)
    b_reduce = noise(streams_of[8], (C,), 0.5, 3.0, (), jnp.float32)
    layer_scale = jnp.clip(jnp.exp(jax.random.uniform(streams_of[9], (C,), jnp.float32, math.log(0.2), math.log(1.5))), 0.2, 1.5)
    cotangent = noise(streams_of[10], (HEIGHT, WIDTH, C), 1.0, 6.0, ((0, 8), (1, 32)))
    return dict(image=image, conv_weight=conv_weight, conv_bias=conv_bias, layernorm_gain=layernorm_gain, layernorm_bias=layernorm_bias, w_expand=w_expand, b_expand=b_expand, w_reduce=w_reduce, b_reduce=b_reduce, layer_scale=layer_scale, cotangent=cotangent)


def gelu_pair(pre):
    root = pre / math.sqrt(2.0)
    cdf = 0.5 * (1.0 + lax.erf(root))
    return (pre * cdf, cdf + pre * jnp.exp(-0.5 * pre * pre) / math.sqrt(2.0 * math.pi))

def mlp_back(conv_out, grad_out, layernorm_gain, layernorm_bias, w_expand, b_expand, w_reduce, b_reduce, layer_scale):
    channel_mean = lax.optimization_barrier(jnp.mean(conv_out, axis=-1, keepdims=True))
    centered_input = conv_out - channel_mean
    var = lax.optimization_barrier(jnp.mean(centered_input * centered_input, axis=-1, keepdims=True))
    inverse_deviation = lax.rsqrt(var + 1e-06)
    standardized_input = centered_input * inverse_deviation
    normalized_output = (standardized_input * layernorm_gain + layernorm_bias).astype(jnp.bfloat16)
    pre = lax.dot_general(normalized_output, w_expand, (((1,), (1,)), ((), ())), preferred_element_type=jnp.float32) + b_expand
    act, slope = gelu_pair(pre)
    hidden = act.astype(jnp.bfloat16)
    branch = lax.dot_general(hidden, w_reduce, (((1,), (1,)), ((), ())), preferred_element_type=jnp.float32) + b_reduce
    grad_f = grad_out.astype(jnp.float32)
    d_branch = (layer_scale * grad_f).astype(jnp.bfloat16)
    d_hidden = jnp.dot(d_branch, w_reduce, preferred_element_type=jnp.float32)
    d_pre = (d_hidden * slope).astype(jnp.bfloat16)
    normalized_gradient = jnp.dot(d_pre, w_expand, preferred_element_type=jnp.float32)
    standardized_gradient = normalized_gradient * layernorm_gain
    convolution_gradient = (standardized_gradient - lax.optimization_barrier(jnp.mean(standardized_gradient, axis=-1, keepdims=True)) - standardized_input * lax.optimization_barrier(jnp.mean(standardized_gradient * standardized_input, axis=-1, keepdims=True))) * inverse_deviation
    heads = (lax.optimization_barrier(jnp.sum(grad_f * branch, axis=0)), lax.optimization_barrier(jnp.sum(d_branch.astype(jnp.float32), axis=0)), lax.optimization_barrier(jnp.sum(d_pre.astype(jnp.float32), axis=0)))
    trailing_parts = (lax.optimization_barrier(jnp.sum(normalized_gradient * standardized_input, axis=0)), lax.optimization_barrier(jnp.sum(normalized_gradient, axis=0)))
    term_expand = lax.dot_general(d_pre, normalized_output, (((0,), (0,)), ((), ())), preferred_element_type=jnp.float32)
    term_reduce = lax.dot_general(d_branch, hidden, (((0,), (0,)), ((), ())), preferred_element_type=jnp.float32)
    return (convolution_gradient, term_expand, term_reduce, heads, trailing_parts)

def reference(image, conv_weight, conv_bias, layernorm_gain, layernorm_bias, w_expand, b_expand, w_reduce, b_reduce, layer_scale, cotangent):
    rows, cols, chans = image.shape
    padded = jnp.pad(image, ((3, 3), (3, 3), (0, 0)))
    conv_out = jnp.zeros((rows, cols, chans), jnp.float32) + conv_bias
    for i in range(KS):
        for j in range(KS):
            conv_out = conv_out + conv_weight[i, j] * padded[i:i + rows, j:j + cols].astype(jnp.float32)

    def one_row(carry, inputs):
        acc_expand, acc_reduce, acc_heads, acc_tails = carry
        conv_row, grad_row = inputs
        convolution_gradient, t_expand, t_reduce, heads, trailing_parts = mlp_back(conv_row, grad_row, layernorm_gain, layernorm_bias, w_expand, b_expand, w_reduce, b_reduce, layer_scale)
        acc_heads = tuple((a + b for a, b in zip(acc_heads, heads)))
        acc_tails = tuple((a + b for a, b in zip(acc_tails, trailing_parts)))
        return ((acc_expand + t_expand, acc_reduce + t_reduce, acc_heads, acc_tails), convolution_gradient)
    zero_c = jnp.zeros((chans,), jnp.float32)
    zero_f = jnp.zeros((w_expand.shape[0],), jnp.float32)
    init = (jnp.zeros(w_expand.shape, jnp.float32), jnp.zeros(w_reduce.shape, jnp.float32), (zero_c, zero_c, zero_f), (zero_c, zero_c))
    carry, convolution_gradient = lax.scan(one_row, init, (conv_out, cotangent))
    acc_expand, acc_reduce, heads, trailing_parts = carry
    d_pad = jnp.pad(convolution_gradient, ((3, 3), (3, 3), (0, 0)))
    grad_image = cotangent.astype(jnp.float32)
    taps = []
    for i in range(KS):
        for j in range(KS):
            grad_image = grad_image + conv_weight[i, j] * d_pad[6 - i:6 - i + rows, 6 - j:6 - j + cols]
            taps.append(lax.optimization_barrier(jnp.sum(padded[i:i + rows, j:j + cols].astype(jnp.float32) * convolution_gradient, axis=(0, 1))))
    scale = 1.0 / math.sqrt(rows * cols)
    grad_conv_weight = jnp.stack(taps).reshape(KS, KS, chans) * scale
    grad_conv_bias = lax.optimization_barrier(jnp.sum(convolution_gradient, axis=(0, 1))) * scale
    return (grad_image, acc_expand * scale, acc_reduce * scale, grad_conv_weight, grad_conv_bias, trailing_parts[0] * scale, trailing_parts[1] * scale, heads[2] * scale, heads[1] * scale, heads[0] * scale)
```

```python
import math

import jax
import jax.numpy as jnp
from jax import lax
from jax.sharding import Mesh
from jax.sharding import PartitionSpec as P

KS = 7
AXES = ("zl", "y", "zh", "x", "c")
SIZES = (2, 4, 4, 4, 2)
ROW = ("zl", "y")
COL = ("zh", "x", "c")
BF = jnp.bfloat16
F32 = jnp.float32


def spot_z(z):
    return (z % 2) * 4 + z // 2


def same(i):
    return i


def axis_of(name):
    if name == "z":
        me = lax.axis_index("zh") * 2 + lax.axis_index("zl")
        return ("zl", "zh"), 8, spot_z, me
    n = SIZES[AXES.index(name)]
    return name, n, same, lax.axis_index(name)


def send_by(v, name, k):
    axes, n, spot, _ = axis_of(name)
    return lax.ppermute(v, axes, [(spot(i), spot((i + k) % n)) for i in range(n)])


def scatter_sum(v, name, dim):
    _, n, _, me = axis_of(name)
    acc = lax.dynamic_index_in_dim(v, me, dim, keepdims=False).astype(F32)
    for k in range(1, n):
        part = lax.dynamic_index_in_dim(v, lax.rem(me + k, n), dim, keepdims=False)
        acc = acc + send_by(part, name, k).astype(F32)
    return acc


def exchange_sum(v, name):
    _, n, _, _ = axis_of(name)
    acc = v
    for k in range(1, n):
        acc = acc + send_by(v, name, k)
    return acc


def gather_all(v, name):
    _, n, _, me = axis_of(name)
    parts = [v] + [send_by(v, name, k) for k in range(1, n)]
    both = jnp.stack(parts[::-1] * 2)
    return lax.dynamic_slice_in_dim(both, n - 1 - me, n, axis=0)


def with_halo(x, w):
    rows, cols, _ = x.shape
    n_row = lax.axis_size(ROW)
    n_col = lax.axis_size(COL)

    def row_shift(v, d):
        return lax.ppermute(v, ROW, [(i, i + d) for i in range(n_row) if 0 <= i + d < n_row])

    def col_shift(v, d):
        return lax.ppermute(v, COL, [(i, i + d) for i in range(n_col) if 0 <= i + d < n_col])

    def both_shift(v, dr, dc):
        pairs = [
            (r * n_col + c, (r + dr) * n_col + c + dc)
            for r in range(n_row)
            for c in range(n_col)
            if 0 <= r + dr < n_row and 0 <= c + dc < n_col
        ]
        return lax.ppermute(v, AXES, pairs)

    north = row_shift(x[rows - w :], 1)
    south = row_shift(x[:w], -1)
    west = col_shift(x[:, cols - w :], 1)
    east = col_shift(x[:, :w], -1)
    nw = both_shift(x[rows - w :, cols - w :], 1, 1)
    ne = both_shift(x[rows - w :, :w], 1, -1)
    sw = both_shift(x[:w, cols - w :], -1, 1)
    se = both_shift(x[:w, :w], -1, -1)
    top = jnp.concatenate([nw, north, ne], axis=1)
    mid = jnp.concatenate([west, x, east], axis=1)
    low = jnp.concatenate([sw, south, se], axis=1)
    return jnp.concatenate([top, mid, low], axis=0)


def gelu_pair(pre):
    root = pre / math.sqrt(2.0)
    cdf = 0.5 * (1.0 + lax.erf(root))
    return (pre * cdf, cdf + pre * jnp.exp(-0.5 * pre * pre) / math.sqrt(2.0 * math.pi))


def unit_order(w, per):
    rest = w.shape[1:]
    v = w.reshape((2, 4, 4, 4, 2, per) + rest)
    v = v.transpose((4, 3, 1, 2, 0, 5) + tuple(range(6, 6 + len(rest))))
    return v.reshape((2, w.shape[0] // 2) + rest)


def near_last(v):
    me = lax.axis_index("c")
    return jnp.concatenate(
        [lax.dynamic_index_in_dim(v, 1 - me, 0, False), lax.dynamic_index_in_dim(v, me, 0, False)],
        axis=0,
    )


def tdot(a, b):
    return lax.dot_general(a, b, (((0,), (0,)), ((), ())), preferred_element_type=F32)


def on_device(
    image,
    conv_weight,
    conv_bias,
    layernorm_gain,
    layernorm_bias,
    w_expand,
    b_expand,
    w_reduce,
    b_reduce,
    layer_scale,
    cotangent,
):
    rows, cols, chans = image.shape
    hid = w_expand.shape[0]
    half = hid // 2
    per = hid // 256
    scale = 1.0 / math.sqrt(rows * cols * 256)
    padded = with_halo(image, 3)
    w_in = near_last(unit_order(w_expand, per))
    w_out = near_last(unit_order(w_reduce.T, per))
    bias_in = near_last(unit_order(b_expand, per))
    conv_out = jnp.zeros((rows, cols, chans), F32) + conv_bias
    for i in range(KS):
        for j in range(KS):
            conv_out = conv_out + conv_weight[i, j] * padded[i : i + rows, j : j + cols].astype(F32)
    flat = conv_out.reshape(rows * cols, chans)
    channel_mean = jnp.mean(flat, axis=-1, keepdims=True)
    centered = flat - channel_mean
    var = jnp.mean(centered * centered, axis=-1, keepdims=True)
    rstd = lax.rsqrt(var + 1e-06)
    xhat = centered * rstd
    normed = (xhat * layernorm_gain + layernorm_bias).astype(BF)
    pre = (
        lax.dot_general(normed, w_in, (((1,), (1,)), ((), ())), preferred_element_type=F32)
        + bias_in
    )
    act, slope = gelu_pair(pre)
    hidden = act.astype(BF)
    grad_f = cotangent.reshape(rows * cols, chans).astype(F32)
    d_branch = (layer_scale * grad_f).astype(BF)

    def first_step(left, right):
        far = tdot(left[:, :half], right).astype(BF)
        come = send_by(far, "c", 1)
        return (tdot(left[:, half:], right) + come.astype(F32)).astype(BF)

    t_reduce = first_step(hidden, d_branch)
    t_reduce = t_reduce.reshape(4, 4, 8 * per, chans)
    t_reduce = scatter_sum(t_reduce, "y", 1).astype(BF)
    t_reduce = scatter_sum(t_reduce, "x", 0).astype(BF)

    d_hidden = lax.dot_general(
        d_branch, w_out, (((1,), (1,)), ((), ())), preferred_element_type=F32
    )
    d_pre = (d_hidden * slope).astype(BF)
    t_expand = first_step(d_pre, normed)
    t_expand = t_expand.reshape(4, 4, 8 * per, chans)
    t_expand = scatter_sum(t_expand, "x", 0).astype(BF)
    t_expand = scatter_sum(t_expand, "y", 0).astype(BF)
    both = jnp.stack([t_expand, t_reduce]).reshape(2, 8, per, chans)
    both = scatter_sum(both, "z", 1) * scale

    branch = jnp.dot(hidden, w_out, preferred_element_type=F32) + b_reduce
    d_normed = jnp.dot(d_pre, w_in, preferred_element_type=F32)
    d_xhat = d_normed * layernorm_gain
    d_flat = (
        d_xhat
        - jnp.mean(d_xhat, axis=-1, keepdims=True)
        - xhat * jnp.mean(d_xhat * xhat, axis=-1, keepdims=True)
    ) * rstd
    d_conv = d_flat.reshape(rows, cols, chans)
    d_pad = with_halo(d_conv.astype(BF), 3)

    sum_pre = jnp.sum(d_pre.astype(F32), axis=0, keepdims=True)
    me = lax.axis_index("c")
    halves = sum_pre.reshape(2, half)
    halves = jnp.where(me == 0, halves[::-1], halves)
    sum_pre = (
        halves.reshape(2, 4, 4, 4, 2, per).transpose(4, 2, 3, 1, 0, 5).reshape(hid // chans, chans)
    )
    early = [
        jnp.sum(d_normed * xhat, axis=0, keepdims=True),
        jnp.sum(d_normed, axis=0, keepdims=True),
        jnp.sum(d_branch.astype(F32), axis=0, keepdims=True),
        jnp.sum(grad_f * branch, axis=0, keepdims=True),
        sum_pre,
    ]
    taps = []
    for i in range(KS):
        for j in range(KS):
            taps.append(
                jnp.sum(
                    padded[i : i + rows, j : j + cols].astype(F32) * d_conv, axis=(0, 1)
                )[None]
            )
    taps.append(jnp.sum(d_flat, axis=0, keepdims=True))
    small = jnp.concatenate(taps + early, axis=0) * scale
    used = small.shape[0]
    total = -(-used // 64) * 64
    small = jnp.pad(small, ((0, total - used), (0, 0))).reshape(2, 4, total // 8, chans)
    small = scatter_sum(small, "c", 0)
    small = scatter_sum(small, "x", 0)
    small = exchange_sum(small, "y")
    small = exchange_sum(small, "z")
    small = gather_all(small, "x").reshape(total // 2, chans)
    small = gather_all(small, "c").reshape(total, chans)

    grad_image = cotangent.astype(F32)
    for i in range(KS):
        for j in range(KS):
            grad_image = grad_image + conv_weight[i, j] * d_pad[
                6 - i : 6 - i + rows, 6 - j : 6 - j + cols
            ].astype(F32)
    kk = KS * KS
    return (
        grad_image,
        both[0],
        both[1].T,
        small[:kk].reshape(KS, KS, chans),
        small[kk],
        small[kk + 1],
        small[kk + 2],
        small[kk + 5 : kk + 5 + hid // chans].reshape(hid),
        small[kk + 3],
        small[kk + 4],
    )


def solution(mesh):
    grid = Mesh(mesh.devices.reshape(SIZES), AXES)
    tile = P(ROW, COL, None)
    one = P()
    in_specs = (tile,) + (one,) * 9 + (tile,)
    out_specs = (tile, P(AXES, None), P(None, AXES)) + (one,) * 7
    return jax.shard_map(
        on_device, mesh=grid, in_specs=in_specs, out_specs=out_specs, check_vma=False
    )
```

```python
import itertools
import math

import jax
import jax.numpy as jnp
from jax import lax
from jax.sharding import Mesh
from jax.sharding import PartitionSpec as P

KS = 7
AXES = ("zl", "y", "zh", "x", "c")
SIZES = (2, 4, 4, 4, 2)
ROW = ("zl", "y")
COL = ("zh", "x", "c")
BF = jnp.bfloat16
F32 = jnp.float32


def spot_z(z):
    return (z % 2) * 4 + z // 2


def core_pairs(k, lead):
    pairs = []
    for spot in itertools.product(*(range(n) for n in SIZES)):
        to = list(spot)
        at = AXES.index(lead[spot[-1]])
        to[at] = (to[at] + k) % SIZES[at]
        pairs.append((flat_index(spot), flat_index(to)))
    return pairs


def flat_index(spot):
    out = 0
    for i, n in zip(spot, SIZES):
        out = out * n + i
    return out


def split_sum(v, small, lead, dims):
    core = lax.axis_index("c")
    me = [lax.axis_index(name) for name in lead]
    chans = v.shape[-1]

    def pick(k):
        parts = [
            lax.dynamic_index_in_dim(v, lax.rem(me[s] + k, 4), dims[s], keepdims=False).reshape(
                -1, chans
            )
            for s in range(2)
        ]
        return jnp.where(core == 0, parts[0], parts[1])

    count = small.shape[0]
    low = small.astype(BF)
    acc = pick(0).astype(F32)
    sums = low.astype(F32)
    for k in range(1, 4):
        sent = jnp.concatenate([low, pick(k)], axis=0)
        got = lax.ppermute(sent, AXES, core_pairs(k, lead)).astype(F32)
        sums = sums + got[:count]
        acc = acc + got[count:]
    return acc, sums


def z_sum(v, small):
    count = small.shape[0]
    low = small.astype(BF)
    zl = lax.axis_index("zl")
    zh = lax.axis_index("zh")
    acc = lax.dynamic_index_in_dim(v, zl, 0, False)
    acc = lax.dynamic_index_in_dim(acc, zh, 0, False).astype(F32)
    sums = low.astype(F32)
    z = zh * 2 + zl
    for k in range(1, 8):
        to = lax.rem(z + k, 8)
        part = lax.dynamic_index_in_dim(v, lax.rem(to, 2), 0, False)
        part = lax.dynamic_index_in_dim(part, to // 2, 0, False)
        sent = jnp.concatenate([low, part], axis=0)
        pairs = [(spot_z(i), spot_z((i + k) % 8)) for i in range(8)]
        got = lax.ppermute(sent, ("zl", "zh"), pairs).astype(F32)
        sums = sums + got[:count]
        acc = acc + got[count:]
    return acc, sums


def core_swap(v):
    return lax.ppermute(v, "c", [(0, 1), (1, 0)])


def with_halo(x, w):
    rows, cols, _ = x.shape
    n_row = lax.axis_size(ROW)
    n_col = lax.axis_size(COL)

    def row_shift(v, d):
        return lax.ppermute(v, ROW, [(i, i + d) for i in range(n_row) if 0 <= i + d < n_row])

    def col_shift(v, d):
        return lax.ppermute(v, COL, [(i, i + d) for i in range(n_col) if 0 <= i + d < n_col])

    def both_shift(v, dr, dc):
        pairs = [
            (r * n_col + c, (r + dr) * n_col + c + dc)
            for r in range(n_row)
            for c in range(n_col)
            if 0 <= r + dr < n_row and 0 <= c + dc < n_col
        ]
        return lax.ppermute(v, AXES, pairs)

    north = row_shift(x[rows - w :], 1)
    south = row_shift(x[:w], -1)
    west = col_shift(x[:, cols - w :], 1)
    east = col_shift(x[:, :w], -1)
    nw = both_shift(x[rows - w :, cols - w :], 1, 1)
    ne = both_shift(x[rows - w :, :w], 1, -1)
    sw = both_shift(x[:w, cols - w :], -1, 1)
    se = both_shift(x[:w, :w], -1, -1)
    top = jnp.concatenate([nw, north, ne], axis=1)
    mid = jnp.concatenate([west, x, east], axis=1)
    low = jnp.concatenate([sw, south, se], axis=1)
    return jnp.concatenate([top, mid, low], axis=0)


def gelu_pair(pre):
    root = pre / math.sqrt(2.0)
    cdf = 0.5 * (1.0 + lax.erf(root))
    return (pre * cdf, cdf + pre * jnp.exp(-0.5 * pre * pre) / math.sqrt(2.0 * math.pi))


def tdot(a, b):
    return lax.dot_general(a, b, (((0,), (0,)), ((), ())), preferred_element_type=F32)


def on_device(
    image,
    conv_weight,
    conv_bias,
    layernorm_gain,
    layernorm_bias,
    w_expand,
    b_expand,
    w_reduce,
    b_reduce,
    layer_scale,
    cotangent,
):
    rows, cols, chans = image.shape
    hid = w_expand.shape[0]
    per = hid // 256
    scale = 1.0 / math.sqrt(rows * cols * 256)
    first = lax.axis_index("c") == 0
    padded = with_halo(image, 3)
    conv_out = jnp.zeros((rows, cols, chans), F32) + conv_bias
    for i in range(KS):
        for j in range(KS):
            conv_out = conv_out + conv_weight[i, j] * padded[i : i + rows, j : j + cols].astype(F32)
    flat = conv_out.reshape(rows * cols, chans)
    channel_mean = jnp.mean(flat, axis=-1, keepdims=True)
    centered = flat - channel_mean
    var = jnp.mean(centered * centered, axis=-1, keepdims=True)
    rstd = lax.rsqrt(var + 1e-06)
    xhat = centered * rstd
    normed = (xhat * layernorm_gain + layernorm_bias).astype(BF)
    pre = (
        lax.dot_general(normed, w_expand, (((1,), (1,)), ((), ())), preferred_element_type=F32)
        + b_expand
    )
    act, slope = gelu_pair(pre)
    hidden = act.astype(BF)
    grad_f = cotangent.reshape(rows * cols, chans).astype(F32)
    d_branch = (layer_scale * grad_f).astype(BF)
    d_hidden = jnp.dot(d_branch, w_reduce, preferred_element_type=F32)
    d_pre = (d_hidden * slope).astype(BF)

    far = tdot(jnp.where(first, hidden, d_pre), jnp.where(first, d_branch, normed)).astype(BF)
    come = core_swap(far)
    near = tdot(jnp.where(first, d_pre, hidden), jnp.where(first, normed, d_branch))
    term = (near + come.astype(F32)).astype(BF).reshape(2, 4, 4, 4, 2 * per, chans)

    branch = (
        lax.dot_general(hidden, w_reduce, (((1,), (1,)), ((), ())), preferred_element_type=F32)
        + b_reduce
    )
    d_normed = jnp.dot(d_pre, w_expand, preferred_element_type=F32)
    d_xhat = d_normed * layernorm_gain
    d_flat = (
        d_xhat
        - jnp.mean(d_xhat, axis=-1, keepdims=True)
        - xhat * jnp.mean(d_xhat * xhat, axis=-1, keepdims=True)
    ) * rstd
    d_conv = d_flat.reshape(rows, cols, chans)

    sums = []
    for i in range(KS):
        for j in range(KS):
            sums.append(
                jnp.sum(padded[i : i + rows, j : j + cols].astype(F32) * d_conv, axis=(0, 1))[None]
            )
    sums += [
        jnp.sum(d_flat, axis=0, keepdims=True),
        jnp.sum(d_normed * xhat, axis=0, keepdims=True),
        jnp.sum(d_normed, axis=0, keepdims=True),
        jnp.sum(d_branch.astype(F32), axis=0, keepdims=True),
        jnp.sum(grad_f * branch, axis=0, keepdims=True),
        jnp.sum(d_pre.astype(F32), axis=0, keepdims=True).reshape(hid // chans, chans),
    ]
    small = jnp.concatenate(sums, axis=0) * scale
    total = -(-small.shape[0] // 32) * 32
    small = jnp.pad(small, ((0, total - small.shape[0]), (0, 0)))
    lower, upper = small[: total // 2], small[total // 2 :]
    small = jnp.where(first, lower, upper) + core_swap(jnp.where(first, upper, lower))

    term, small = split_sum(term, small, ("x", "y"), (3, 1))
    term = term.astype(BF).reshape(2, 4, 4, 2 * per, chans)
    term, small = split_sum(term, small, ("y", "x"), (1, 2))
    term = term.astype(BF).reshape(2, 4, 2 * per, chans)
    term, small = z_sum(term, small)
    term = term * scale
    top, low = term[:per], term[per:]
    got = core_swap(jnp.concatenate([small, jnp.where(first, low, top)], axis=0))
    keep = jnp.where(first, top, low)
    other, got = got[: total // 2], got[total // 2 :]
    small = jnp.concatenate(
        [jnp.where(first, small, other), jnp.where(first, other, small)], axis=0
    )
    grad_expand = jnp.where(first, keep, got)
    grad_reduce = jnp.where(first, got, keep).T

    d_pad = with_halo(d_conv.astype(BF), 3)
    grad_image = cotangent.astype(F32)
    for i in range(KS):
        for j in range(KS):
            grad_image = grad_image + conv_weight[i, j] * d_pad[
                6 - i : 6 - i + rows, 6 - j : 6 - j + cols
            ].astype(F32)
    kk = KS * KS
    return (
        grad_image,
        grad_expand,
        grad_reduce,
        small[:kk].reshape(KS, KS, chans),
        small[kk],
        small[kk + 1],
        small[kk + 2],
        small[kk + 5 : kk + 5 + hid // chans].reshape(hid),
        small[kk + 3],
        small[kk + 4],
    )


def solution(mesh):
    grid = Mesh(mesh.devices.reshape(SIZES), AXES)
    tile = P(ROW, COL, None)
    one = P()
    in_specs = (tile,) + (one,) * 9 + (tile,)
    out_specs = (tile, P(AXES, None), P(None, AXES)) + (one,) * 7
    return jax.shard_map(
        on_device, mesh=grid, in_specs=in_specs, out_specs=out_specs, check_vma=False
    )
```

```python
import functools
import itertools
import math

import jax
import jax.numpy as jnp
from jax import lax
from jax.experimental import pallas as pl
from jax.experimental.pallas import tpu as pltpu
from jax.sharding import Mesh
from jax.sharding import PartitionSpec as P

KS = 7
AXES = ("zl", "y", "zh", "x", "c")
SIZES = (2, 4, 4, 4, 2)
ROW = ("zl", "y")
COL = ("zh", "x", "c")
BF = jnp.bfloat16
F32 = jnp.float32


def spot_z(z):
    return (z % 2) * 4 + z // 2


def core_pairs(k, lead):
    pairs = []
    for spot in itertools.product(*(range(n) for n in SIZES)):
        to = list(spot)
        at = AXES.index(lead[spot[-1]])
        to[at] = (to[at] + k) % SIZES[at]
        pairs.append((flat_index(spot), flat_index(to)))
    return pairs


def flat_index(spot):
    out = 0
    for i, n in zip(spot, SIZES):
        out = out * n + i
    return out


def split_send(v, small, lead, dims):
    core = lax.axis_index("c")
    me = [lax.axis_index(name) for name in lead]
    chans = v.shape[-1]

    def pick(k):
        parts = [
            lax.dynamic_index_in_dim(v, lax.rem(me[s] + k, 4), dims[s], keepdims=False).reshape(
                -1, chans
            )
            for s in range(2)
        ]
        return jnp.where(core == 0, parts[0], parts[1])

    low = small.astype(BF)
    return [jnp.concatenate([low, pick(k)], axis=0) for k in range(4)]


def split_move(moved, lead):
    return [lax.ppermute(moved[k], AXES, core_pairs(k, lead)) for k in range(1, 4)]


def split_add(moved, got, count):
    def add(part):
        out = part(moved[0]).astype(F32)
        for v in got:
            out = out + part(v).astype(F32)
        return out

    return add(lambda v: v[count:]), add(lambda v: v[:count])


def z_sum(v, small):
    count = small.shape[0]
    low = small.astype(BF)
    zl = lax.axis_index("zl")
    zh = lax.axis_index("zh")
    acc = lax.dynamic_index_in_dim(v, zl, 0, False)
    acc = lax.dynamic_index_in_dim(acc, zh, 0, False).astype(F32)
    sums = low.astype(F32)
    z = zh * 2 + zl
    for k in range(1, 8):
        to = lax.rem(z + k, 8)
        part = lax.dynamic_index_in_dim(v, lax.rem(to, 2), 0, False)
        part = lax.dynamic_index_in_dim(part, to // 2, 0, False)
        sent = jnp.concatenate([low, part], axis=0)
        pairs = [(spot_z(i), spot_z((i + k) % 8)) for i in range(8)]
        got = lax.ppermute(sent, ("zl", "zh"), pairs)
        sums = sums + got[:count].astype(F32)
        acc = acc + got[count:].astype(F32)
    return acc, sums


def core_swap(v):
    return lax.ppermute(v, "c", [(0, 1), (1, 0)])


def with_halo(x, w):
    rows, cols, _ = x.shape

    def shift(v, axes, d):
        n = lax.axis_size(axes)
        return lax.ppermute(v, axes, [(i, i + d) for i in range(n) if 0 <= i + d < n])

    west = shift(x[:, cols - w :], COL, 1)
    east = shift(x[:, :w], COL, -1)
    x = jnp.concatenate([west, x, east], axis=1)
    north = shift(x[rows - w :], ROW, 1)
    south = shift(x[:w], ROW, -1)
    return jnp.concatenate([north, x, south], axis=0)


def gelu_pair(pre):
    root = pre / math.sqrt(2.0)
    cdf = 0.5 * (1.0 + lax.erf(root))
    return (pre * cdf, cdf + pre * jnp.exp(-0.5 * pre * pre) / math.sqrt(2.0 * math.pi))


def tdot(a, b):
    return lax.dot_general(a, b, (((0,), (0,)), ((), ())), preferred_element_type=F32)


def backward_kernel(
    scale, pad_ref, conv_ref, dn_ref, br_ref, cot_ref, pre_ref, par_ref, small_ref, out_ref, im, dd, acc
):
    rows, cols, chans = conv_ref.shape
    lanes = 128
    blocks = chans // lanes
    high, wide, _ = pad_ref.shape
    gain = par_ref[0:1, :]
    bias = par_ref[1:2, :]
    layer = par_ref[2:3, :]
    acc[...] = jnp.zeros_like(acc)

    def spread(r, _):
        row = pad_ref[r].astype(F32)
        for b in range(blocks):
            im[b, r, 0:wide, :] = row[:, b * lanes : (b + 1) * lanes]
        return 0

    lax.fori_loop(0, high, spread, 0)

    def fold(v):
        out = v[0:8]
        for t in range(8, cols, 8):
            out = out + v[t : t + 8]
        return out

    def norm(r, _):
        v = conv_ref[r]
        v = v - jnp.mean(v, axis=-1, keepdims=True)
        rstd = lax.rsqrt(jnp.mean(v * v, axis=-1, keepdims=True) + 1e-06)
        xhat = v * rstd
        dn = dn_ref[r]
        dx = dn * gain
        d = (
            dx
            - jnp.mean(dx, axis=-1, keepdims=True)
            - xhat * jnp.mean(dx * xhat, axis=-1, keepdims=True)
        ) * rstd
        out_ref[r] = d.astype(BF)
        for b in range(blocks):
            dd[b, r] = d[:, b * lanes : (b + 1) * lanes]
        g = cot_ref[r].astype(F32)
        acc[0] += fold(d)
        acc[1] += fold(dn * xhat)
        acc[2] += fold(dn)
        acc[3] += fold((g * layer).astype(BF).astype(F32))
        acc[4] += fold(g * (br_ref[r] + bias))
        return 0

    lax.fori_loop(0, rows, norm, 0)
    kk = KS * KS
    for t in range(5):
        small_ref[kk + t : kk + t + 1, :] = jnp.sum(acc[t], axis=0, keepdims=True) * scale
    n_pre = pre_ref.shape[0]
    small_ref[kk + 5 : kk + 5 + n_pre, :] = pre_ref[...] * scale
    left = small_ref.shape[0] - (kk + 5 + n_pre)
    if left:
        small_ref[kk + 5 + n_pre :, :] = jnp.zeros((left, chans), F32)

    part = 8

    def taps(b, _):
        at = pl.ds(pl.multiple_of(b * lanes, lanes), lanes)
        for j in range(KS):
            total = [jnp.zeros((8, lanes), F32) for _ in range(KS)]
            for p0 in range(0, rows, part):
                size = min(part, rows - p0)
                held = [dd[b, p0 + p] for p in range(size)]
                for r in range(size + KS - 1):
                    s = im[b, p0 + r, j : j + cols, :]
                    for i in range(KS):
                        if 0 <= r - i < size:
                            total[i] = total[i] + fold(held[r - i] * s)
            for i in range(KS):
                t = KS * i + j
                small_ref[t : t + 1, at] = jnp.sum(total[i], axis=0, keepdims=True) * scale
        return 0

    lax.fori_loop(0, blocks, taps, 0)


def backward(scale, padded, conv_out, d_normed, branch, cotangent, sum_pre, params):
    rows, cols, chans = conv_out.shape
    used = KS * KS + 5 + sum_pre.shape[0]
    total = -(-used // 32) * 32
    blocks = chans // 128
    return pl.pallas_call(
        functools.partial(backward_kernel, scale),
        out_shape=(
            jax.ShapeDtypeStruct((total, chans), F32),
            jax.ShapeDtypeStruct((rows, cols, chans), BF),
        ),
        scratch_shapes=[
            pltpu.VMEM((blocks, rows + KS - 1, cols + 8, 128), F32),
            pltpu.VMEM((blocks, rows, cols, 128), F32),
            pltpu.VMEM((8, 8, chans), F32),
        ],
        compiler_params=pltpu.CompilerParams(vmem_limit_bytes=40 * 1024 * 1024),
        cost_estimate=pl.CostEstimate(
            flops=2 * KS * KS * rows * cols * chans, bytes_accessed=8 * 1024 * 1024, transcendentals=0
        ),
        name="backward",
    )(padded, conv_out, d_normed, branch, cotangent, sum_pre, params)


def on_device(
    image,
    conv_weight,
    conv_bias,
    layernorm_gain,
    layernorm_bias,
    w_expand,
    b_expand,
    w_reduce,
    b_reduce,
    layer_scale,
    cotangent,
):
    rows, cols, chans = image.shape
    hid = w_expand.shape[0]
    per = hid // 256
    scale = 1.0 / math.sqrt(rows * cols * 256)
    first = lax.axis_index("c") == 0
    padded = with_halo(image, 3)
    conv_out = jnp.zeros((rows, cols, chans), F32) + conv_bias
    for i in range(KS):
        for j in range(KS):
            conv_out = conv_out + conv_weight[i, j] * padded[i : i + rows, j : j + cols].astype(F32)
    flat = conv_out.reshape(rows * cols, chans)
    channel_mean = jnp.mean(flat, axis=-1, keepdims=True)
    centered = flat - channel_mean
    var = jnp.mean(centered * centered, axis=-1, keepdims=True)
    rstd = lax.rsqrt(var + 1e-06)
    xhat = centered * rstd
    normed = (xhat * layernorm_gain + layernorm_bias).astype(BF)
    pre = (
        lax.dot_general(normed, w_expand, (((1,), (1,)), ((), ())), preferred_element_type=F32)
        + b_expand
    )
    act, slope = gelu_pair(pre)
    hidden = act.astype(BF)
    grad_f = cotangent.reshape(rows * cols, chans).astype(F32)
    d_branch = (layer_scale * grad_f).astype(BF)
    d_hidden = jnp.dot(d_branch, w_reduce, preferred_element_type=F32)
    d_pre = (d_hidden * slope).astype(BF)

    far = tdot(jnp.where(first, hidden, d_pre), jnp.where(first, d_branch, normed)).astype(BF)
    come = core_swap(far)
    near = tdot(jnp.where(first, d_pre, hidden), jnp.where(first, normed, d_branch))
    near = lax.optimization_barrier(near)
    term = (near + come.astype(F32)).astype(BF).reshape(2, 4, 4, 4, 2 * per, chans)

    branch = lax.dot_general(
        hidden, w_reduce, (((1,), (1,)), ((), ())), preferred_element_type=F32
    )
    d_normed = jnp.dot(d_pre, w_expand, preferred_element_type=F32)
    sum_pre = jnp.sum(d_pre.astype(F32), axis=0).reshape(hid // chans, chans)
    params = jnp.stack([layernorm_gain, b_reduce, layer_scale] + [layer_scale] * 5)
    shape = (rows, cols, chans)
    small, d_conv = backward(
        scale,
        padded,
        conv_out,
        d_normed.reshape(shape),
        branch.reshape(shape),
        cotangent,
        sum_pre,
        params,
    )
    total = small.shape[0]
    lower, upper = small[: total // 2], small[total // 2 :]
    small = jnp.where(first, lower, upper) + core_swap(jnp.where(first, upper, lower))

    moved = split_send(term, small, ("x", "y"), (3, 1))
    d_pad = with_halo(d_conv, 3)
    grad_image = cotangent.astype(F32)
    for i in range(KS):
        for j in range(KS):
            grad_image = grad_image + conv_weight[i, j] * d_pad[
                6 - i : 6 - i + rows, 6 - j : 6 - j + cols
            ].astype(F32)
    got = split_move(moved, ("x", "y"))
    got, grad_image = lax.optimization_barrier((got, grad_image))
    term, small = split_add(moved, got, small.shape[0])
    term = term.astype(BF).reshape(2, 4, 4, 2 * per, chans)
    moved = split_send(term, small, ("y", "x"), (1, 2))
    term, small = split_add(moved, split_move(moved, ("y", "x")), small.shape[0])
    term = term.astype(BF).reshape(2, 4, 2 * per, chans)
    term, small = z_sum(term, small)
    term = term * scale
    top, low = term[:per], term[per:]
    got = core_swap(jnp.concatenate([small, jnp.where(first, low, top)], axis=0))
    keep = jnp.where(first, top, low)
    other, got = got[: total // 2], got[total // 2 :]
    small = jnp.concatenate(
        [jnp.where(first, small, other), jnp.where(first, other, small)], axis=0
    )
    grad_expand = jnp.where(first, keep, got)
    grad_reduce = jnp.where(first, got, keep).T

    kk = KS * KS
    return (
        grad_image,
        grad_expand,
        grad_reduce,
        small[:kk].reshape(KS, KS, chans),
        small[kk],
        small[kk + 1],
        small[kk + 2],
        small[kk + 5 : kk + 5 + hid // chans].reshape(hid),
        small[kk + 3],
        small[kk + 4],
    )


def solution(mesh):
    grid = Mesh(mesh.devices.reshape(SIZES), AXES)
    tile = P(ROW, COL, None)
    one = P()
    in_specs = (tile,) + (one,) * 9 + (tile,)
    out_specs = (tile, P(AXES, None), P(None, AXES)) + (one,) * 7
    return jax.shard_map(
        on_device, mesh=grid, in_specs=in_specs, out_specs=out_specs, check_vma=False
    )
```

```python
import functools
import itertools
import math

import jax
import jax.numpy as jnp
from jax import lax
from jax.experimental import pallas as pl
from jax.experimental.pallas import tpu as pltpu
from jax.sharding import Mesh
from jax.sharding import PartitionSpec as P

KS = 7
AXES = ("zl", "y", "zh", "x", "c")
SIZES = (2, 4, 4, 4, 2)
ROW = ("zl", "y")
COL = ("zh", "x", "c")
BF = jnp.bfloat16
F32 = jnp.float32


def core_pairs(k, lead):
    pairs = []
    for spot in itertools.product(*(range(n) for n in SIZES)):
        to = list(spot)
        at = AXES.index(lead[spot[-1]])
        to[at] = (to[at] + k) % SIZES[at]
        pairs.append((flat_index(spot), flat_index(to)))
    return pairs


def flat_index(spot):
    out = 0
    for i, n in zip(spot, SIZES):
        out = out * n + i
    return out


def split_send(v, small, lead, dims):
    core = lax.axis_index("c")
    me = [lax.axis_index(name) for name in lead]
    chans = v.shape[-1]

    def pick(k):
        parts = [
            lax.dynamic_index_in_dim(v, lax.rem(me[s] + k, 4), dims[s], keepdims=False).reshape(
                -1, chans
            )
            for s in range(2)
        ]
        return jnp.where(core == 0, parts[0], parts[1])

    low = small.astype(BF)
    return [jnp.concatenate([low, pick(k)], axis=0) for k in range(4)]


def split_move(moved, lead):
    return [lax.ppermute(moved[k], AXES, core_pairs(k, lead)) for k in range(1, 4)]


def split_add(moved, got, count):
    def add(part):
        out = part(moved[0]).astype(F32)
        for v in got:
            out = out + part(v).astype(F32)
        return out

    return add(lambda v: v[count:]), add(lambda v: v[:count])


def z_sum(v, small):
    count, chans = small.shape
    low = small.astype(BF)
    zl = lax.axis_index("zl")
    zh = lax.axis_index("zh")
    away = lax.dynamic_index_in_dim(v, 1 - zl, 0, False).reshape(-1, chans)
    near = lax.dynamic_index_in_dim(v, zl, 0, False).reshape(-1, chans)
    got = lax.ppermute(jnp.concatenate([low, away], axis=0), "zl", [(0, 1), (1, 0)])
    low = (low.astype(F32) + got[:count].astype(F32)).astype(BF)
    v = (near.astype(F32) + got[count:].astype(F32)).astype(BF).reshape(v.shape[1:])
    acc = lax.dynamic_index_in_dim(v, zh, 0, False).astype(F32)
    sums = low.astype(F32)
    for k in range(1, 4):
        part = lax.dynamic_index_in_dim(v, lax.rem(zh + k, 4), 0, False)
        sent = jnp.concatenate([low, part], axis=0)
        got = lax.ppermute(sent, "zh", [(i, (i + k) % 4) for i in range(4)])
        sums = sums + got[:count].astype(F32)
        acc = acc + got[count:].astype(F32)
    return acc, sums


def core_swap(v):
    return lax.ppermute(v, "c", [(0, 1), (1, 0)])


def shift(v, axes, d):
    n = lax.axis_size(axes)
    return lax.ppermute(v, axes, [(i, i + d) for i in range(n) if 0 <= i + d < n])


def halo_columns(x, w):
    west = shift(x[:, x.shape[1] - w :], COL, 1)
    east = shift(x[:, :w], COL, -1)
    return jnp.concatenate([west, x, east], axis=1)


def halo_rows(x, w):
    north = shift(x[x.shape[0] - w :], ROW, 1)
    south = shift(x[:w], ROW, -1)
    return jnp.concatenate([north, x, south], axis=0)


def gelu_pair(pre):
    root = pre / math.sqrt(2.0)
    cdf = 0.5 * (1.0 + lax.erf(root))
    return (pre * cdf, cdf + pre * jnp.exp(-0.5 * pre * pre) / math.sqrt(2.0 * math.pi))


def tdot(a, b):
    return lax.dot_general(a, b, (((0,), (0,)), ((), ())), preferred_element_type=F32)


def backward_kernel(
    scale, pad_ref, conv_ref, dn_ref, br_ref, cot_ref, pre_ref, par_ref, small_ref, out_ref, im, dd, acc
):
    rows, cols, chans = conv_ref.shape
    lanes = 128
    blocks = chans // lanes
    high, wide, _ = pad_ref.shape
    gain = par_ref[0:1, :]
    bias = par_ref[1:2, :]
    layer = par_ref[2:3, :]
    acc[...] = jnp.zeros_like(acc)

    def spread(r, _):
        row = pad_ref[r].astype(F32)
        for b in range(blocks):
            im[b, r, 0:wide, :] = row[:, b * lanes : (b + 1) * lanes]
        return 0

    lax.fori_loop(0, high, spread, 0)

    def fold(v):
        out = v[0:8]
        for t in range(8, cols, 8):
            out = out + v[t : t + 8]
        return out

    def norm(r, _):
        v = conv_ref[r]
        v = v - jnp.mean(v, axis=-1, keepdims=True)
        rstd = lax.rsqrt(jnp.mean(v * v, axis=-1, keepdims=True) + 1e-06)
        xhat = v * rstd
        dn = dn_ref[r]
        dx = dn * gain
        d = (
            dx
            - jnp.mean(dx, axis=-1, keepdims=True)
            - xhat * jnp.mean(dx * xhat, axis=-1, keepdims=True)
        ) * rstd
        out_ref[r] = d.astype(BF)
        for b in range(blocks):
            dd[b, r] = d[:, b * lanes : (b + 1) * lanes]
        g = cot_ref[r].astype(F32)
        acc[0] += fold(d)
        acc[1] += fold(dn * xhat)
        acc[2] += fold(dn)
        acc[3] += fold((g * layer).astype(BF).astype(F32))
        acc[4] += fold(g * (br_ref[r] + bias))
        return 0

    lax.fori_loop(0, rows, norm, 0)
    kk = KS * KS
    for t in range(5):
        small_ref[kk + t : kk + t + 1, :] = jnp.sum(acc[t], axis=0, keepdims=True) * scale
    n_pre = pre_ref.shape[0]
    small_ref[kk + 5 : kk + 5 + n_pre, :] = pre_ref[...] * scale
    left = small_ref.shape[0] - (kk + 5 + n_pre)
    if left:
        small_ref[kk + 5 + n_pre :, :] = jnp.zeros((left, chans), F32)

    part = 8

    def taps(b, _):
        at = pl.ds(pl.multiple_of(b * lanes, lanes), lanes)
        for j in range(KS):
            total = [jnp.zeros((8, lanes), F32) for _ in range(KS)]
            for p0 in range(0, rows, part):
                size = min(part, rows - p0)
                held = [dd[b, p0 + p] for p in range(size)]
                for r in range(size + KS - 1):
                    s = im[b, p0 + r, j : j + cols, :]
                    for i in range(KS):
                        if 0 <= r - i < size:
                            total[i] = total[i] + fold(held[r - i] * s)
            for i in range(KS):
                t = KS * i + j
                small_ref[t : t + 1, at] = jnp.sum(total[i], axis=0, keepdims=True) * scale
        return 0

    lax.fori_loop(0, blocks, taps, 0)


def backward(scale, padded, conv_out, d_normed, branch, cotangent, sum_pre, params):
    rows, cols, chans = conv_out.shape
    used = KS * KS + 5 + sum_pre.shape[0]
    total = -(-used // 32) * 32
    blocks = chans // 128
    return pl.pallas_call(
        functools.partial(backward_kernel, scale),
        out_shape=(
            jax.ShapeDtypeStruct((total, chans), F32),
            jax.ShapeDtypeStruct((rows, cols, chans), BF),
        ),
        scratch_shapes=[
            pltpu.VMEM((blocks, rows + KS - 1, cols + 8, 128), F32),
            pltpu.VMEM((blocks, rows, cols, 128), F32),
            pltpu.VMEM((8, 8, chans), F32),
        ],
        compiler_params=pltpu.CompilerParams(vmem_limit_bytes=40 * 1024 * 1024),
        cost_estimate=pl.CostEstimate(
            flops=2 * KS * KS * rows * cols * chans, bytes_accessed=8 * 1024 * 1024, transcendentals=0
        ),
        name="backward",
    )(padded, conv_out, d_normed, branch, cotangent, sum_pre, params)


def chunk_kernel(at_ref, pre_ref, hid_ref, normed_ref, db_ref, come_ref, low_ref, *outs):
    unit = hid_ref.shape[1] // 16
    core = at_ref[0]
    me = (at_ref[1], at_ref[2])
    group = pl.program_id(0)
    count = low_ref.shape[0]
    first = core == 0
    lhs = jnp.where(first, pre_ref[...], hid_ref[...])
    rhs = jnp.where(first, normed_ref[...], db_ref[...])
    v = lax.dot_general(lhs, rhs, (((0,), (0,)), ((), ())), preferred_element_type=F32)
    v = v + come_ref[...].astype(F32)

    @pl.when(group == 0)
    def _():
        for out in outs:
            out[0:count, :] = low_ref[...]

    def store(k, row, value):
        value = value.astype(BF)
        rows = pl.ds(pl.multiple_of(count + row, 16), 2 * unit)
        for n in range(4):

            @pl.when(k == n)
            def _(n=n):
                outs[n][rows, :] = value

    def part(zh, x):
        t = zh * 4 + x
        return v[t * unit : (t + 1) * unit]

    @pl.when(first)
    def _():
        for x in range(4):
            k = lax.rem(x + 4 - me[0], 4)
            for zh in (0, 2):
                value = jnp.concatenate([part(zh, x), part(zh + 1, x)], axis=0)
                store(k, (group * 4 + zh) * unit, value)

    @pl.when(core == 1)
    def _():
        k = lax.rem(lax.rem(group, 4) + 4 - me[1], 4)
        for zh in range(4):
            for x in (0, 2):
                t = zh * 4 + x
                store(k, ((group // 4) * 16 + t) * unit, v[t * unit : (t + 2) * unit])


def chunks(d_pre, hidden, normed, d_branch, come, low):
    pixels, hid = hidden.shape
    chans = normed.shape[1]
    count = low.shape[0]
    wide = hid // 8
    at = jnp.stack([lax.axis_index("c"), lax.axis_index("x"), lax.axis_index("y")]).astype(
        jnp.int32
    )
    whole = pl.BlockSpec((pixels, chans), lambda g: (0, 0))
    columns = pl.BlockSpec((pixels, wide), lambda g: (0, g))
    rows = count + hid // 4
    return pl.pallas_call(
        chunk_kernel,
        grid=(8,),
        in_specs=[
            pl.BlockSpec(memory_space=pltpu.SMEM),
            columns,
            columns,
            whole,
            whole,
            pl.BlockSpec((wide, chans), lambda g: (g, 0)),
            pl.BlockSpec((count, chans), lambda g: (0, 0)),
        ],
        out_specs=[pl.BlockSpec((rows, chans), lambda g: (0, 0))] * 4,
        out_shape=[jax.ShapeDtypeStruct((rows, chans), BF)] * 4,
        compiler_params=pltpu.CompilerParams(vmem_limit_bytes=40 * 1024 * 1024),
        cost_estimate=pl.CostEstimate(
            flops=2 * pixels * hid * chans, bytes_accessed=18 * 1024 * 1024, transcendentals=0
        ),
        name="chunks",
    )(at, d_pre, hidden, normed, d_branch, come, low)


def on_device(
    image,
    conv_weight,
    conv_bias,
    layernorm_gain,
    layernorm_bias,
    w_expand,
    b_expand,
    w_reduce,
    b_reduce,
    layer_scale,
    cotangent,
):
    rows, cols, chans = image.shape
    hid = w_expand.shape[0]
    per = hid // 256
    scale = 1.0 / math.sqrt(rows * cols * 256)
    first = lax.axis_index("c") == 0
    padded = halo_rows(halo_columns(image, 3), 3)
    conv_out = jnp.zeros((rows, cols, chans), F32) + conv_bias
    for i in range(KS):
        for j in range(KS):
            conv_out = conv_out + conv_weight[i, j] * padded[i : i + rows, j : j + cols].astype(F32)
    flat = conv_out.reshape(rows * cols, chans)
    channel_mean = jnp.mean(flat, axis=-1, keepdims=True)
    centered = flat - channel_mean
    var = jnp.mean(centered * centered, axis=-1, keepdims=True)
    rstd = lax.rsqrt(var + 1e-06)
    xhat = centered * rstd
    normed = (xhat * layernorm_gain + layernorm_bias).astype(BF)
    pre = (
        lax.dot_general(normed, w_expand, (((1,), (1,)), ((), ())), preferred_element_type=F32)
        + b_expand
    )
    act, slope = gelu_pair(pre)
    hidden = act.astype(BF)
    grad_f = cotangent.reshape(rows * cols, chans).astype(F32)
    d_branch = (layer_scale * grad_f).astype(BF)
    d_hidden = jnp.dot(d_branch, w_reduce, preferred_element_type=F32)
    d_pre = (d_hidden * slope).astype(BF)

    far = tdot(jnp.where(first, hidden, d_pre), jnp.where(first, d_branch, normed)).astype(BF)
    come = core_swap(far)
    branch = lax.dot_general(
        hidden, w_reduce, (((1,), (1,)), ((), ())), preferred_element_type=F32
    )
    d_normed = jnp.dot(d_pre, w_expand, preferred_element_type=F32)
    sum_pre = jnp.sum(d_pre.astype(F32), axis=0).reshape(hid // chans, chans)
    params = jnp.stack([layernorm_gain, b_reduce, layer_scale] + [layer_scale] * 5)
    shape = (rows, cols, chans)
    small, d_conv = backward(
        scale,
        padded,
        conv_out,
        d_normed.reshape(shape),
        branch.reshape(shape),
        cotangent,
        sum_pre,
        params,
    )
    total = small.shape[0]
    lower, upper = small[: total // 2], small[total // 2 :]
    small = jnp.where(first, lower, upper) + core_swap(jnp.where(first, upper, lower))

    moved = list(chunks(d_pre, hidden, normed, d_branch, come, small.astype(BF)))
    wide = halo_columns(d_conv, 3)
    wide, moved[0] = lax.optimization_barrier((wide, moved[0]))
    d_pad = halo_rows(wide, 3)
    grad_image = cotangent.astype(F32)
    for i in range(KS):
        for j in range(KS):
            grad_image = grad_image + conv_weight[i, j] * d_pad[
                6 - i : 6 - i + rows, 6 - j : 6 - j + cols
            ].astype(F32)
    got = split_move(moved, ("x", "y"))
    got, grad_image = lax.optimization_barrier((got, grad_image))
    term, small = split_add(moved, got, small.shape[0])
    term = term.astype(BF).reshape(2, 4, 4, 2 * per, chans)
    moved = split_send(term, small, ("y", "x"), (1, 2))
    term, small = split_add(moved, split_move(moved, ("y", "x")), small.shape[0])
    term = term.astype(BF).reshape(2, 4, 2 * per, chans)
    term, small = z_sum(term, small)
    term = term * scale
    top, low = term[:per], term[per:]
    got = core_swap(jnp.concatenate([small, jnp.where(first, low, top)], axis=0))
    keep = jnp.where(first, top, low)
    other, got = got[: total // 2], got[total // 2 :]
    small = jnp.concatenate(
        [jnp.where(first, small, other), jnp.where(first, other, small)], axis=0
    )
    grad_expand = jnp.where(first, keep, got)
    grad_reduce = jnp.where(first, got, keep).T

    kk = KS * KS
    return (
        grad_image,
        grad_expand,
        grad_reduce,
        small[:kk].reshape(KS, KS, chans),
        small[kk],
        small[kk + 1],
        small[kk + 2],
        small[kk + 5 : kk + 5 + hid // chans].reshape(hid),
        small[kk + 3],
        small[kk + 4],
    )


def solution(mesh):
    grid = Mesh(mesh.devices.reshape(SIZES), AXES)
    tile = P(ROW, COL, None)
    one = P()
    in_specs = (tile,) + (one,) * 9 + (tile,)
    out_specs = (tile, P(AXES, None), P(None, AXES)) + (one,) * 7
    return jax.shard_map(
        on_device, mesh=grid, in_specs=in_specs, out_specs=out_specs, check_vma=False
    )
```

```python
import functools
import itertools
import math

import jax
import jax.numpy as jnp
from jax import lax
from jax.experimental import pallas as pl
from jax.experimental.pallas import tpu as pltpu
from jax.sharding import Mesh
from jax.sharding import PartitionSpec as P

KS = 7
AXES = ("zl", "y", "zh", "x", "c")
SIZES = (2, 4, 4, 4, 2)
ROW = ("zl", "y")
COL = ("zh", "x", "c")
BF = jnp.bfloat16
F32 = jnp.float32


def core_pairs(k, lead):
    pairs = []
    for spot in itertools.product(*(range(n) for n in SIZES)):
        to = list(spot)
        at = AXES.index(lead[spot[-1]])
        to[at] = (to[at] + k) % SIZES[at]
        pairs.append((flat_index(spot), flat_index(to)))
    return pairs


def flat_index(spot):
    out = 0
    for i, n in zip(spot, SIZES):
        out = out * n + i
    return out


def split_send(v, small, lead, dims):
    core = lax.axis_index("c")
    me = [lax.axis_index(name) for name in lead]
    chans = v.shape[-1]

    def pick(k):
        parts = [
            lax.dynamic_index_in_dim(v, lax.rem(me[s] + k, 4), dims[s], keepdims=False).reshape(
                -1, chans
            )
            for s in range(2)
        ]
        return jnp.where(core == 0, parts[0], parts[1])

    low = small.astype(BF)
    return [jnp.concatenate([low, pick(k)], axis=0) for k in range(4)]


def split_move(moved, lead):
    return [lax.ppermute(moved[k], AXES, core_pairs(k, lead)) for k in range(1, 4)]


def split_add(moved, got, count):
    def add(part):
        out = part(moved[0]).astype(F32)
        for v in got:
            out = out + part(v).astype(F32)
        return out

    return add(lambda v: v[count:]), add(lambda v: v[:count])


def add_all(parts):
    out = parts[0].astype(F32)
    for v in parts[1:]:
        out = out + v.astype(F32)
    return out


def z_sum(v, small):
    count, chans = small.shape
    zl = lax.axis_index("zl")
    zh = lax.axis_index("zh")
    away = lax.dynamic_index_in_dim(v, 1 - zl, 0, False).reshape(-1, chans)
    near = lax.dynamic_index_in_dim(v, zl, 0, False).reshape(-1, chans)
    low = small.astype(BF)
    got = zl_swap(away)
    low = add_all([low] + split_move([low] * 4, ("x", "y"))).astype(BF)
    v = (near.astype(F32) + got.astype(F32)).astype(BF).reshape(v.shape[1:])
    acc = lax.dynamic_index_in_dim(v, zh, 0, False).astype(F32)
    sums = low.astype(F32)
    for k in range(1, 4):
        part = lax.dynamic_index_in_dim(v, lax.rem(zh + k, 4), 0, False)
        sent = jnp.concatenate([low, part], axis=0)
        got = lax.ppermute(sent, "zh", [(i, (i + k) % 4) for i in range(4)])
        sums = sums + got[:count].astype(F32)
        acc = acc + got[count:].astype(F32)
    return acc, sums


def zl_swap(v):
    return lax.ppermute(v, "zl", [(0, 1), (1, 0)])


def core_swap(v):
    return lax.ppermute(v, "c", [(0, 1), (1, 0)])


def shift(v, axes, d):
    n = lax.axis_size(axes)
    return lax.ppermute(v, axes, [(i, i + d) for i in range(n) if 0 <= i + d < n])


def halo_columns(x, w):
    west = shift(x[:, x.shape[1] - w :], COL, 1)
    east = shift(x[:, :w], COL, -1)
    return jnp.concatenate([west, x, east], axis=1)


def halo_rows(x, w):
    north = shift(x[x.shape[0] - w :], ROW, 1)
    south = shift(x[:w], ROW, -1)
    return jnp.concatenate([north, x, south], axis=0)


def gelu_pair(pre):
    root = pre / math.sqrt(2.0)
    cdf = 0.5 * (1.0 + lax.erf(root))
    return (pre * cdf, cdf + pre * jnp.exp(-0.5 * pre * pre) / math.sqrt(2.0 * math.pi))


def tdot(a, b):
    return lax.dot_general(a, b, (((0,), (0,)), ((), ())), preferred_element_type=F32)


def backward_kernel(
    scale, pad_ref, conv_ref, dn_ref, br_ref, cot_ref, pre_ref, par_ref, small_ref, out_ref, im, dd, acc
):
    rows, cols, chans = conv_ref.shape
    lanes = 128
    blocks = chans // lanes
    high, wide, _ = pad_ref.shape
    gain = par_ref[0:1, :]
    bias = par_ref[1:2, :]
    layer = par_ref[2:3, :]
    acc[...] = jnp.zeros_like(acc)

    def spread(r, _):
        row = pad_ref[r].astype(F32)
        for b in range(blocks):
            im[b, r, 0:wide, :] = row[:, b * lanes : (b + 1) * lanes]
        return 0

    lax.fori_loop(0, high, spread, 0)

    def fold(v):
        out = v[0:8]
        for t in range(8, cols, 8):
            out = out + v[t : t + 8]
        return out

    def norm(r, _):
        v = conv_ref[r]
        v = v - jnp.mean(v, axis=-1, keepdims=True)
        rstd = lax.rsqrt(jnp.mean(v * v, axis=-1, keepdims=True) + 1e-06)
        xhat = v * rstd
        dn = dn_ref[r]
        dx = dn * gain
        d = (
            dx
            - jnp.mean(dx, axis=-1, keepdims=True)
            - xhat * jnp.mean(dx * xhat, axis=-1, keepdims=True)
        ) * rstd
        out_ref[r] = d.astype(BF)
        for b in range(blocks):
            dd[b, r] = d[:, b * lanes : (b + 1) * lanes]
        g = cot_ref[r].astype(F32)
        acc[0] += fold(d)
        acc[1] += fold(dn * xhat)
        acc[2] += fold(dn)
        acc[3] += fold((g * layer).astype(BF).astype(F32))
        acc[4] += fold(g * (br_ref[r] + bias))
        return 0

    lax.fori_loop(0, rows, norm, 0)
    kk = KS * KS
    for t in range(5):
        small_ref[kk + t : kk + t + 1, :] = jnp.sum(acc[t], axis=0, keepdims=True) * scale
    n_pre = pre_ref.shape[0]
    small_ref[kk + 5 : kk + 5 + n_pre, :] = pre_ref[...] * scale
    left = small_ref.shape[0] - (kk + 5 + n_pre)
    if left:
        small_ref[kk + 5 + n_pre :, :] = jnp.zeros((left, chans), F32)

    part = 8

    def taps(b, _):
        at = pl.ds(pl.multiple_of(b * lanes, lanes), lanes)
        for j in range(KS):
            total = [jnp.zeros((8, lanes), F32) for _ in range(KS)]
            for p0 in range(0, rows, part):
                size = min(part, rows - p0)
                held = [dd[b, p0 + p] for p in range(size)]
                for r in range(size + KS - 1):
                    s = im[b, p0 + r, j : j + cols, :]
                    for i in range(KS):
                        if 0 <= r - i < size:
                            total[i] = total[i] + fold(held[r - i] * s)
            for i in range(KS):
                t = KS * i + j
                small_ref[t : t + 1, at] = jnp.sum(total[i], axis=0, keepdims=True) * scale
        return 0

    lax.fori_loop(0, blocks, taps, 0)


def backward(scale, padded, conv_out, d_normed, branch, cotangent, sum_pre, params):
    rows, cols, chans = conv_out.shape
    used = KS * KS + 5 + sum_pre.shape[0]
    total = -(-used // 32) * 32
    blocks = chans // 128
    return pl.pallas_call(
        functools.partial(backward_kernel, scale),
        out_shape=(
            jax.ShapeDtypeStruct((total, chans), F32),
            jax.ShapeDtypeStruct((rows, cols, chans), BF),
        ),
        scratch_shapes=[
            pltpu.VMEM((blocks, rows + KS - 1, cols + 8, 128), F32),
            pltpu.VMEM((blocks, rows, cols, 128), F32),
            pltpu.VMEM((8, 8, chans), F32),
        ],
        compiler_params=pltpu.CompilerParams(vmem_limit_bytes=40 * 1024 * 1024),
        cost_estimate=pl.CostEstimate(
            flops=2 * KS * KS * rows * cols * chans, bytes_accessed=8 * 1024 * 1024, transcendentals=0
        ),
        name="backward",
    )(padded, conv_out, d_normed, branch, cotangent, sum_pre, params)


def chunk_kernel(at_ref, pre_ref, hid_ref, normed_ref, db_ref, come_ref, *outs):
    unit = hid_ref.shape[1] // 16
    core = at_ref[0]
    me = (at_ref[1], at_ref[2])
    group = pl.program_id(0)
    first = core == 0
    lhs = jnp.where(first, pre_ref[...], hid_ref[...])
    rhs = jnp.where(first, normed_ref[...], db_ref[...])
    v = lax.dot_general(lhs, rhs, (((0,), (0,)), ((), ())), preferred_element_type=F32)
    v = v + come_ref[...].astype(F32)

    def store(k, row, value):
        value = value.astype(BF)
        rows = pl.ds(pl.multiple_of(row, 16), 2 * unit)
        for n in range(4):

            @pl.when(k == n)
            def _(n=n):
                outs[n][rows, :] = value

    def part(zh, x):
        t = zh * 4 + x
        return v[t * unit : (t + 1) * unit]

    @pl.when(first)
    def _():
        for x in range(4):
            k = lax.rem(x + 4 - me[0], 4)
            for zh in (0, 2):
                value = jnp.concatenate([part(zh, x), part(zh + 1, x)], axis=0)
                store(k, (group * 4 + zh) * unit, value)

    @pl.when(core == 1)
    def _():
        k = lax.rem(lax.rem(group, 4) + 4 - me[1], 4)
        for zh in range(4):
            for x in (0, 2):
                t = zh * 4 + x
                store(k, ((group // 4) * 16 + t) * unit, v[t * unit : (t + 2) * unit])


def chunks(d_pre, hidden, normed, d_branch, come):
    pixels, hid = hidden.shape
    chans = normed.shape[1]
    wide = hid // 8
    at = jnp.stack([lax.axis_index("c"), lax.axis_index("x"), lax.axis_index("y")]).astype(
        jnp.int32
    )
    whole = pl.BlockSpec((pixels, chans), lambda g: (0, 0))
    columns = pl.BlockSpec((pixels, wide), lambda g: (0, g))
    rows = hid // 4
    return pl.pallas_call(
        chunk_kernel,
        grid=(8,),
        in_specs=[
            pl.BlockSpec(memory_space=pltpu.SMEM),
            columns,
            columns,
            whole,
            whole,
            pl.BlockSpec((wide, chans), lambda g: (g, 0)),
        ],
        out_specs=[pl.BlockSpec((rows, chans), lambda g: (0, 0))] * 4,
        out_shape=[pltpu.HBM((rows, chans), BF)] * 4,
        compiler_params=pltpu.CompilerParams(vmem_limit_bytes=40 * 1024 * 1024),
        cost_estimate=pl.CostEstimate(
            flops=2 * pixels * hid * chans, bytes_accessed=18 * 1024 * 1024, transcendentals=0
        ),
        name="chunks",
    )(at, d_pre, hidden, normed, d_branch, come)


def on_device(
    image,
    conv_weight,
    conv_bias,
    layernorm_gain,
    layernorm_bias,
    w_expand,
    b_expand,
    w_reduce,
    b_reduce,
    layer_scale,
    cotangent,
):
    rows, cols, chans = image.shape
    hid = w_expand.shape[0]
    per = hid // 256
    scale = 1.0 / math.sqrt(rows * cols * 256)
    first = lax.axis_index("c") == 0
    padded = halo_rows(halo_columns(image, 3), 3)
    conv_out = jnp.zeros((rows, cols, chans), F32) + conv_bias
    for i in range(KS):
        for j in range(KS):
            conv_out = conv_out + conv_weight[i, j] * padded[i : i + rows, j : j + cols].astype(F32)
    flat = conv_out.reshape(rows * cols, chans)
    channel_mean = jnp.mean(flat, axis=-1, keepdims=True)
    centered = flat - channel_mean
    var = jnp.mean(centered * centered, axis=-1, keepdims=True)
    rstd = lax.rsqrt(var + 1e-06)
    xhat = centered * rstd
    normed = (xhat * layernorm_gain + layernorm_bias).astype(BF)
    pre = (
        lax.dot_general(normed, w_expand, (((1,), (1,)), ((), ())), preferred_element_type=F32)
        + b_expand
    )
    act, slope = gelu_pair(pre)
    hidden = act.astype(BF)
    grad_f = cotangent.reshape(rows * cols, chans).astype(F32)
    d_branch = (layer_scale * grad_f).astype(BF)
    d_hidden = jnp.dot(d_branch, w_reduce, preferred_element_type=F32)
    d_pre = (d_hidden * slope).astype(BF)

    far = tdot(jnp.where(first, hidden, d_pre), jnp.where(first, d_branch, normed)).astype(BF)
    come = core_swap(far)
    branch = lax.dot_general(
        hidden, w_reduce, (((1,), (1,)), ((), ())), preferred_element_type=F32
    )
    d_normed = jnp.dot(d_pre, w_expand, preferred_element_type=F32)
    sum_pre = jnp.sum(d_pre.astype(F32), axis=0).reshape(hid // chans, chans)
    params = jnp.stack([layernorm_gain, b_reduce, layer_scale] + [layer_scale] * 5)
    shape = (rows, cols, chans)

    moved = list(chunks(d_pre, hidden, normed, d_branch, come))
    got = split_move(moved, ("x", "y"))
    d_normed, moved[0] = lax.optimization_barrier((d_normed, moved[0]))
    small, d_conv = backward(
        scale,
        padded,
        conv_out,
        d_normed.reshape(shape),
        branch.reshape(shape),
        cotangent,
        sum_pre,
        params,
    )
    total = small.shape[0]
    lower, upper = small[: total // 2], small[total // 2 :]
    small = jnp.where(first, lower, upper) + core_swap(jnp.where(first, upper, lower))
    low = small.astype(BF)
    small = low.astype(F32) + zl_swap(low).astype(F32)
    d_pad = halo_rows(halo_columns(d_conv, 3), 3)
    got, small, d_pad = lax.optimization_barrier((got, small, d_pad))
    term = add_all([moved[0]] + got).astype(BF).reshape(2, 4, 4, 2 * per, chans)

    moved = split_send(term, small, ("y", "x"), (1, 2))
    got = split_move(moved, ("y", "x"))
    grad_image = cotangent.astype(F32)
    for i in range(KS):
        for j in range(KS):
            grad_image = grad_image + conv_weight[i, j] * d_pad[
                6 - i : 6 - i + rows, 6 - j : 6 - j + cols
            ].astype(F32)
    got, grad_image = lax.optimization_barrier((got, grad_image))
    term, small = split_add(moved, got, small.shape[0])
    term = term.astype(BF).reshape(2, 4, 2 * per, chans)
    term, small = z_sum(term, small)
    term = term * scale
    top, low = term[:per], term[per:]
    got = core_swap(jnp.concatenate([small, jnp.where(first, low, top)], axis=0))
    keep = jnp.where(first, top, low)
    other, got = got[: total // 2], got[total // 2 :]
    small = jnp.concatenate(
        [jnp.where(first, small, other), jnp.where(first, other, small)], axis=0
    )
    grad_expand = jnp.where(first, keep, got)
    grad_reduce = jnp.where(first, got, keep).T

    kk = KS * KS
    return (
        grad_image,
        grad_expand,
        grad_reduce,
        small[:kk].reshape(KS, KS, chans),
        small[kk],
        small[kk + 1],
        small[kk + 2],
        small[kk + 5 : kk + 5 + hid // chans].reshape(hid),
        small[kk + 3],
        small[kk + 4],
    )


def solution(mesh):
    grid = Mesh(mesh.devices.reshape(SIZES), AXES)
    tile = P(ROW, COL, None)
    one = P()
    in_specs = (tile,) + (one,) * 9 + (tile,)
    out_specs = (tile, P(AXES, None), P(None, AXES)) + (one,) * 7
    return jax.shard_map(
        on_device, mesh=grid, in_specs=in_specs, out_specs=out_specs, check_vma=False
    )
```

```python
import functools
import itertools
import math

import jax
import jax.numpy as jnp
from jax import lax
from jax.experimental import pallas as pl
from jax.experimental.pallas import tpu as pltpu
from jax.sharding import Mesh
from jax.sharding import PartitionSpec as P

KS = 7
AXES = ("zl", "y", "zh", "x", "c")
SIZES = (2, 4, 4, 4, 2)
ROW = ("zl", "y")
COL = ("zh", "x", "c")
BF = jnp.bfloat16
F32 = jnp.float32


def core_pairs(k, lead):
    pairs = []
    for spot in itertools.product(*(range(n) for n in SIZES)):
        to = list(spot)
        at = AXES.index(lead[spot[-1]])
        to[at] = (to[at] + k) % SIZES[at]
        pairs.append((flat_index(spot), flat_index(to)))
    return pairs


def flat_index(spot):
    out = 0
    for i, n in zip(spot, SIZES):
        out = out * n + i
    return out


def split_send(v, small, lead, dims):
    core = lax.axis_index("c")
    me = [lax.axis_index(name) for name in lead]
    chans = v.shape[-1]

    def pick(k):
        parts = [
            lax.dynamic_index_in_dim(v, lax.rem(me[s] + k, 4), dims[s], keepdims=False).reshape(
                -1, chans
            )
            for s in range(2)
        ]
        return jnp.where(core == 0, parts[0], parts[1])

    low = small.astype(BF)
    return [jnp.concatenate([low, pick(k)], axis=0) for k in range(4)]


def split_move(moved, lead):
    return [lax.ppermute(moved[k], AXES, core_pairs(k, lead)) for k in range(1, 4)]


def split_add(moved, got, count):
    def add(part):
        out = part(moved[0]).astype(F32)
        for v in got:
            out = out + part(v).astype(F32)
        return out

    return add(lambda v: v[count:]), add(lambda v: v[:count])


def add_all(parts):
    out = parts[0].astype(F32)
    for v in parts[1:]:
        out = out + v.astype(F32)
    return out


def z_sum(v, small):
    count, chans = small.shape
    zl = lax.axis_index("zl")
    zh = lax.axis_index("zh")
    away = lax.dynamic_index_in_dim(v, 1 - zl, 0, False).reshape(-1, chans)
    near = lax.dynamic_index_in_dim(v, zl, 0, False).reshape(-1, chans)
    low = small.astype(BF)
    got = zl_swap(away)
    low = add_all([low] + split_move([low] * 4, ("x", "y"))).astype(BF)
    v = (near.astype(F32) + got.astype(F32)).astype(BF).reshape(v.shape[1:])
    acc = lax.dynamic_index_in_dim(v, zh, 0, False).astype(F32)
    sums = low.astype(F32)
    for k in range(1, 4):
        part = lax.dynamic_index_in_dim(v, lax.rem(zh + k, 4), 0, False)
        sent = jnp.concatenate([low, part], axis=0)
        got = lax.ppermute(sent, "zh", [(i, (i + k) % 4) for i in range(4)])
        sums = sums + got[:count].astype(F32)
        acc = acc + got[count:].astype(F32)
    return acc, sums


def zl_swap(v):
    return lax.ppermute(v, "zl", [(0, 1), (1, 0)])


def core_swap(v):
    return lax.ppermute(v, "c", [(0, 1), (1, 0)])


def shift(v, axes, d):
    n = lax.axis_size(axes)
    return lax.ppermute(v, axes, [(i, i + d) for i in range(n) if 0 <= i + d < n])


def halo_columns(x, w):
    west = shift(x[:, x.shape[1] - w :], COL, 1)
    east = shift(x[:, :w], COL, -1)
    return jnp.concatenate([west, x, east], axis=1)


def halo_rows(x, w):
    north = shift(x[x.shape[0] - w :], ROW, 1)
    south = shift(x[:w], ROW, -1)
    return jnp.concatenate([north, x, south], axis=0)


def gelu_pair(pre):
    root = pre / math.sqrt(2.0)
    cdf = 0.5 * (1.0 + lax.erf(root))
    return (pre * cdf, cdf + pre * jnp.exp(-0.5 * pre * pre) / math.sqrt(2.0 * math.pi))


def tdot(a, b):
    return lax.dot_general(a, b, (((0,), (0,)), ((), ())), preferred_element_type=F32)


def backward_kernel(
    scale, pad_ref, conv_ref, dn_ref, br_ref, cot_ref, pre_ref, par_ref, small_ref, out_ref, im, dd, acc
):
    rows, cols, chans = conv_ref.shape
    lanes = 128
    blocks = chans // lanes
    high, wide, _ = pad_ref.shape
    gain = par_ref[0:1, :]
    bias = par_ref[1:2, :]
    layer = par_ref[2:3, :]
    acc[...] = jnp.zeros_like(acc)

    def spread(r, _):
        row = pad_ref[r].astype(F32)
        for b in range(blocks):
            im[b, r, 0:wide, :] = row[:, b * lanes : (b + 1) * lanes]
        return 0

    lax.fori_loop(0, high, spread, 0)

    def fold(v):
        out = v[0:8]
        for t in range(8, cols, 8):
            out = out + v[t : t + 8]
        return out

    def norm(r, _):
        v = conv_ref[r]
        v = v - jnp.mean(v, axis=-1, keepdims=True)
        rstd = lax.rsqrt(jnp.mean(v * v, axis=-1, keepdims=True) + 1e-06)
        xhat = v * rstd
        dn = dn_ref[r]
        dx = dn * gain
        d = (
            dx
            - jnp.mean(dx, axis=-1, keepdims=True)
            - xhat * jnp.mean(dx * xhat, axis=-1, keepdims=True)
        ) * rstd
        out_ref[r] = d.astype(BF)
        for b in range(blocks):
            dd[b, r] = d[:, b * lanes : (b + 1) * lanes]
        g = cot_ref[r].astype(F32)
        acc[0] += fold(d)
        acc[1] += fold(dn * xhat)
        acc[2] += fold(dn)
        acc[3] += fold((g * layer).astype(BF).astype(F32))
        acc[4] += fold(g * (br_ref[r] + bias))
        return 0

    lax.fori_loop(0, rows, norm, 0)
    kk = KS * KS
    for t in range(5):
        small_ref[kk + t : kk + t + 1, :] = jnp.sum(acc[t], axis=0, keepdims=True) * scale
    n_pre = pre_ref.shape[0]
    small_ref[kk + 5 : kk + 5 + n_pre, :] = pre_ref[...] * scale
    left = small_ref.shape[0] - (kk + 5 + n_pre)
    if left:
        small_ref[kk + 5 + n_pre :, :] = jnp.zeros((left, chans), F32)

    part = 8

    def taps(b, _):
        at = pl.ds(pl.multiple_of(b * lanes, lanes), lanes)
        for j in range(KS):
            total = [jnp.zeros((8, lanes), F32) for _ in range(KS)]
            for p0 in range(0, rows, part):
                size = min(part, rows - p0)
                held = [dd[b, p0 + p] for p in range(size)]
                for r in range(size + KS - 1):
                    s = im[b, p0 + r, j : j + cols, :]
                    for i in range(KS):
                        if 0 <= r - i < size:
                            total[i] = total[i] + fold(held[r - i] * s)
            for i in range(KS):
                t = KS * i + j
                small_ref[t : t + 1, at] = jnp.sum(total[i], axis=0, keepdims=True) * scale
        return 0

    lax.fori_loop(0, blocks, taps, 0)


def backward(scale, padded, conv_out, d_normed, branch, cotangent, sum_pre, params):
    rows, cols, chans = conv_out.shape
    used = KS * KS + 5 + sum_pre.shape[0]
    total = -(-used // 32) * 32
    blocks = chans // 128
    return pl.pallas_call(
        functools.partial(backward_kernel, scale),
        out_shape=(
            jax.ShapeDtypeStruct((total, chans), F32),
            jax.ShapeDtypeStruct((rows, cols, chans), BF),
        ),
        scratch_shapes=[
            pltpu.VMEM((blocks, rows + KS - 1, cols + 8, 128), F32),
            pltpu.VMEM((blocks, rows, cols, 128), F32),
            pltpu.VMEM((8, 8, chans), F32),
        ],
        compiler_params=pltpu.CompilerParams(vmem_limit_bytes=40 * 1024 * 1024),
        cost_estimate=pl.CostEstimate(
            flops=2 * KS * KS * rows * cols * chans, bytes_accessed=8 * 1024 * 1024, transcendentals=0
        ),
        name="backward",
    )(padded, conv_out, d_normed, branch, cotangent, sum_pre, params)


def conv_kernel(ahead, pad_ref, w_ref, *refs):
    if ahead:
        par_ref, out_ref, normed_ref, im = refs
    else:
        start_ref, out_ref, im = refs
    rows, cols, chans = out_ref.shape
    high, wide, _ = pad_ref.shape
    lanes = 128
    blocks = chans // lanes
    kk = KS * KS

    def spread(r, _):
        row = pad_ref[r].astype(F32)
        for b in range(blocks):
            im[b, r, 0:wide, :] = row[:, b * lanes : (b + 1) * lanes]
        return 0

    lax.fori_loop(0, high, spread, 0)
    part = 8

    def block(b, _):
        at = pl.ds(pl.multiple_of(b * lanes, lanes), lanes)
        for p0 in range(0, rows, part):
            size = min(part, rows - p0)
            if ahead:
                acc = [jnp.zeros((cols, lanes), F32) + par_ref[0:1, at] for _ in range(size)]
            else:
                acc = [start_ref[p0 + p, :, at].astype(F32) for p in range(size)]
            for j in range(KS):
                spots = [KS * i + j for i in range(KS)]
                w = [
                    w_ref[t : t + 1, at] if ahead else w_ref[kk - 1 - t : kk - t, at]
                    for t in spots
                ]
                for r in range(size + KS - 1):
                    v = im[b, p0 + r, j : j + cols, :]
                    for i in range(KS):
                        if 0 <= r - i < size:
                            acc[r - i] = acc[r - i] + w[i] * v
            for p in range(size):
                out_ref[p0 + p, :, at] = acc[p]
        return 0

    lax.fori_loop(0, blocks, block, 0)
    if ahead:

        def norm(r, _):
            v = out_ref[r]
            v = v - jnp.mean(v, axis=-1, keepdims=True)
            rstd = lax.rsqrt(jnp.mean(v * v, axis=-1, keepdims=True) + 1e-06)
            normed_ref[r] = ((v * rstd) * par_ref[1:2, :] + par_ref[2:3, :]).astype(BF)
            return 0

        lax.fori_loop(0, rows, norm, 0)


def conv(ahead, padded, weights, extra):
    high, wide, chans = padded.shape
    shape = (high - KS + 1, wide - KS + 1, chans)
    out = jax.ShapeDtypeStruct(shape, F32)
    return pl.pallas_call(
        functools.partial(conv_kernel, ahead),
        out_shape=(out, jax.ShapeDtypeStruct(shape, BF)) if ahead else out,
        scratch_shapes=[pltpu.VMEM((chans // 128, high, shape[1] + 8, 128), F32)],
        compiler_params=pltpu.CompilerParams(vmem_limit_bytes=32 * 1024 * 1024),
        cost_estimate=pl.CostEstimate(
            flops=2 * KS * KS * math.prod(shape), bytes_accessed=16 * 1024 * 1024, transcendentals=0
        ),
        name="conv_norm" if ahead else "conv_image",
    )(padded, weights, extra)


def chunk_kernel(at_ref, pre_ref, hid_ref, normed_ref, db_ref, come_ref, *outs):
    unit = hid_ref.shape[1] // 16
    core = at_ref[0]
    me = (at_ref[1], at_ref[2])
    group = pl.program_id(0)
    first = core == 0
    lhs = jnp.where(first, pre_ref[...], hid_ref[...])
    rhs = jnp.where(first, normed_ref[...], db_ref[...])
    v = lax.dot_general(lhs, rhs, (((0,), (0,)), ((), ())), preferred_element_type=F32)
    v = v + come_ref[...].astype(F32)

    def store(k, row, value):
        value = value.astype(BF)
        rows = pl.ds(pl.multiple_of(row, 16), 2 * unit)
        for n in range(4):

            @pl.when(k == n)
            def _(n=n):
                outs[n][rows, :] = value

    def part(zh, x):
        t = zh * 4 + x
        return v[t * unit : (t + 1) * unit]

    @pl.when(first)
    def _():
        for x in range(4):
            k = lax.rem(x + 4 - me[0], 4)
            for zh in (0, 2):
                value = jnp.concatenate([part(zh, x), part(zh + 1, x)], axis=0)
                store(k, (group * 4 + zh) * unit, value)

    @pl.when(core == 1)
    def _():
        k = lax.rem(lax.rem(group, 4) + 4 - me[1], 4)
        for zh in range(4):
            for x in (0, 2):
                t = zh * 4 + x
                store(k, ((group // 4) * 16 + t) * unit, v[t * unit : (t + 2) * unit])


def chunks(d_pre, hidden, normed, d_branch, come):
    pixels, hid = hidden.shape
    chans = normed.shape[1]
    wide = hid // 8
    at = jnp.stack([lax.axis_index("c"), lax.axis_index("x"), lax.axis_index("y")]).astype(
        jnp.int32
    )
    whole = pl.BlockSpec((pixels, chans), lambda g: (0, 0))
    columns = pl.BlockSpec((pixels, wide), lambda g: (0, g))
    rows = hid // 4
    return pl.pallas_call(
        chunk_kernel,
        grid=(8,),
        in_specs=[
            pl.BlockSpec(memory_space=pltpu.SMEM),
            columns,
            columns,
            whole,
            whole,
            pl.BlockSpec((wide, chans), lambda g: (g, 0)),
        ],
        out_specs=[pl.BlockSpec((rows, chans), lambda g: (0, 0))] * 4,
        out_shape=[pltpu.HBM((rows, chans), BF)] * 4,
        compiler_params=pltpu.CompilerParams(vmem_limit_bytes=40 * 1024 * 1024),
        cost_estimate=pl.CostEstimate(
            flops=2 * pixels * hid * chans, bytes_accessed=18 * 1024 * 1024, transcendentals=0
        ),
        name="chunks",
    )(at, d_pre, hidden, normed, d_branch, come)


def on_device(
    image,
    conv_weight,
    conv_bias,
    layernorm_gain,
    layernorm_bias,
    w_expand,
    b_expand,
    w_reduce,
    b_reduce,
    layer_scale,
    cotangent,
):
    rows, cols, chans = image.shape
    hid = w_expand.shape[0]
    per = hid // 256
    scale = 1.0 / math.sqrt(rows * cols * 256)
    first = lax.axis_index("c") == 0
    padded = halo_rows(halo_columns(image, 3), 3)
    kernel = conv_weight.reshape(KS * KS, chans)
    conv_out, normed = conv(
        True,
        padded,
        kernel,
        jnp.stack([conv_bias, layernorm_gain, layernorm_bias] + [layernorm_bias] * 5),
    )
    normed = normed.reshape(rows * cols, chans)
    pre = (
        lax.dot_general(normed, w_expand, (((1,), (1,)), ((), ())), preferred_element_type=F32)
        + b_expand
    )
    act, slope = gelu_pair(pre)
    hidden = act.astype(BF)
    grad_f = cotangent.reshape(rows * cols, chans).astype(F32)
    d_branch = (layer_scale * grad_f).astype(BF)
    d_hidden = jnp.dot(d_branch, w_reduce, preferred_element_type=F32)
    d_pre = (d_hidden * slope).astype(BF)

    far = tdot(jnp.where(first, hidden, d_pre), jnp.where(first, d_branch, normed)).astype(BF)
    come = core_swap(far)
    branch = lax.dot_general(
        hidden, w_reduce, (((1,), (1,)), ((), ())), preferred_element_type=F32
    )
    d_normed = jnp.dot(d_pre, w_expand, preferred_element_type=F32)
    sum_pre = jnp.sum(d_pre.astype(F32), axis=0).reshape(hid // chans, chans)
    params = jnp.stack([layernorm_gain, b_reduce, layer_scale] + [layer_scale] * 5)
    shape = (rows, cols, chans)

    moved = list(chunks(d_pre, hidden, normed, d_branch, come))
    got = split_move(moved, ("x", "y"))
    d_normed, moved[0] = lax.optimization_barrier((d_normed, moved[0]))
    small, d_conv = backward(
        scale,
        padded,
        conv_out,
        d_normed.reshape(shape),
        branch.reshape(shape),
        cotangent,
        sum_pre,
        params,
    )
    total = small.shape[0]
    lower, upper = small[: total // 2], small[total // 2 :]
    small = jnp.where(first, lower, upper) + core_swap(jnp.where(first, upper, lower))
    low = small.astype(BF)
    small = low.astype(F32) + zl_swap(low).astype(F32)
    wide = halo_columns(d_conv, 3)
    d_pad = halo_rows(wide, 3)
    got, small, wide = lax.optimization_barrier((got, small, wide))
    term = add_all([moved[0]] + got).astype(BF).reshape(2, 4, 4, 2 * per, chans)

    moved = split_send(term, small, ("y", "x"), (1, 2))
    got = split_move(moved, ("y", "x"))
    grad_image = conv(False, d_pad, kernel, cotangent)
    got, grad_image = lax.optimization_barrier((got, grad_image))
    term, small = split_add(moved, got, small.shape[0])
    term = term.astype(BF).reshape(2, 4, 2 * per, chans)
    term, small = z_sum(term, small)
    term = term * scale
    top, low = term[:per], term[per:]
    got = core_swap(jnp.concatenate([small, jnp.where(first, low, top)], axis=0))
    keep = jnp.where(first, top, low)
    other, got = got[: total // 2], got[total // 2 :]
    small = jnp.concatenate(
        [jnp.where(first, small, other), jnp.where(first, other, small)], axis=0
    )
    grad_expand = jnp.where(first, keep, got)
    grad_reduce = jnp.where(first, got, keep).T

    kk = KS * KS
    return (
        grad_image,
        grad_expand,
        grad_reduce,
        small[:kk].reshape(KS, KS, chans),
        small[kk],
        small[kk + 1],
        small[kk + 2],
        small[kk + 5 : kk + 5 + hid // chans].reshape(hid),
        small[kk + 3],
        small[kk + 4],
    )


def solution(mesh):
    grid = Mesh(mesh.devices.reshape(SIZES), AXES)
    tile = P(ROW, COL, None)
    one = P()
    in_specs = (tile,) + (one,) * 9 + (tile,)
    out_specs = (tile, P(AXES, None), P(None, AXES)) + (one,) * 7
    return jax.shard_map(
        on_device, mesh=grid, in_specs=in_specs, out_specs=out_specs, check_vma=False
    )
```

```python
import functools
import itertools
import math

import jax
import jax.numpy as jnp
from jax import lax
from jax.experimental import pallas as pl
from jax.experimental.pallas import tpu as pltpu
from jax.sharding import Mesh
from jax.sharding import PartitionSpec as P

KS = 7
AXES = ("zl", "y", "zh", "x", "c")
SIZES = (2, 4, 4, 4, 2)
ROW = ("zl", "y")
COL = ("zh", "x", "c")
BF = jnp.bfloat16
F32 = jnp.float32


def core_pairs(k, lead):
    pairs = []
    for spot in itertools.product(*(range(n) for n in SIZES)):
        to = list(spot)
        at = AXES.index(lead[spot[-1]])
        to[at] = (to[at] + k) % SIZES[at]
        pairs.append((flat_index(spot), flat_index(to)))
    return pairs


def flat_index(spot):
    out = 0
    for i, n in zip(spot, SIZES):
        out = out * n + i
    return out


def split_send(v, small, lead, dims):
    core = lax.axis_index("c")
    me = [lax.axis_index(name) for name in lead]
    chans = v.shape[-1]

    def pick(k):
        parts = [
            lax.dynamic_index_in_dim(v, lax.rem(me[s] + k, 4), dims[s], keepdims=False).reshape(
                -1, chans
            )
            for s in range(2)
        ]
        return jnp.where(core == 0, parts[0], parts[1])

    low = small.astype(BF)
    return [jnp.concatenate([low, pick(k)], axis=0) for k in range(4)]


def split_move(moved, lead):
    return [lax.ppermute(moved[k], AXES, core_pairs(k, lead)) for k in range(1, 4)]


def split_add(moved, got, count):
    def add(part):
        out = part(moved[0]).astype(F32)
        for v in got:
            out = out + part(v).astype(F32)
        return out

    return add(lambda v: v[count:]), add(lambda v: v[:count])


def add_all(parts):
    out = parts[0].astype(F32)
    for v in parts[1:]:
        out = out + v.astype(F32)
    return out


def z_sum(v, small, beside):
    count, chans = small.shape
    zl = lax.axis_index("zl")
    zh = lax.axis_index("zh")
    away = lax.dynamic_index_in_dim(v, 1 - zl, 0, False).reshape(-1, chans)
    near = lax.dynamic_index_in_dim(v, zl, 0, False).reshape(-1, chans)
    low = small.astype(BF)
    got = zl_swap(away)
    others = split_move([low] * 4, ("x", "y"))
    got, others, beside = lax.optimization_barrier((got, others, beside))
    low = add_all([low] + others).astype(BF)
    v = (near.astype(F32) + got.astype(F32)).astype(BF).reshape(v.shape[1:])
    acc = lax.dynamic_index_in_dim(v, zh, 0, False).astype(F32)
    sums = low.astype(F32)
    for k in range(1, 4):
        part = lax.dynamic_index_in_dim(v, lax.rem(zh + k, 4), 0, False)
        sent = jnp.concatenate([low, part], axis=0)
        got = lax.ppermute(sent, "zh", [(i, (i + k) % 4) for i in range(4)])
        sums = sums + got[:count].astype(F32)
        acc = acc + got[count:].astype(F32)
    return acc, sums, beside


def zl_swap(v):
    return lax.ppermute(v, "zl", [(0, 1), (1, 0)])


def core_swap(v):
    return lax.ppermute(v, "c", [(0, 1), (1, 0)])


def shift(v, axes, d):
    n = lax.axis_size(axes)
    return lax.ppermute(v, axes, [(i, i + d) for i in range(n) if 0 <= i + d < n])


def halo_columns(x, w):
    west = shift(x[:, x.shape[1] - w :], COL, 1)
    east = shift(x[:, :w], COL, -1)
    return jnp.concatenate([west, x, east], axis=1)


def halo_rows(x, w):
    north = shift(x[x.shape[0] - w :], ROW, 1)
    south = shift(x[:w], ROW, -1)
    return jnp.concatenate([north, x, south], axis=0)


def gelu_pair(pre):
    root = pre / math.sqrt(2.0)
    cdf = 0.5 * (1.0 + lax.erf(root))
    return (pre * cdf, cdf + pre * jnp.exp(-0.5 * pre * pre) / math.sqrt(2.0 * math.pi))


def tdot(a, b):
    return lax.dot_general(a, b, (((0,), (0,)), ((), ())), preferred_element_type=F32)


def backward_kernel(
    scale, pad_ref, conv_ref, dn_ref, br_ref, cot_ref, pre_ref, par_ref, small_ref, out_ref, im, dd, acc
):
    rows, cols, chans = conv_ref.shape
    lanes = 128
    blocks = chans // lanes
    high, wide, _ = pad_ref.shape
    gain = par_ref[0:1, :]
    bias = par_ref[1:2, :]
    layer = par_ref[2:3, :]
    acc[...] = jnp.zeros_like(acc)

    def spread(r, _):
        row = pad_ref[r].astype(F32)
        for b in range(blocks):
            im[b, r, 0:wide, :] = row[:, b * lanes : (b + 1) * lanes]
        return 0

    lax.fori_loop(0, high, spread, 0)

    def fold(v):
        out = v[0:8]
        for t in range(8, cols, 8):
            out = out + v[t : t + 8]
        return out

    def norm(r, _):
        v = conv_ref[r]
        v = v - jnp.mean(v, axis=-1, keepdims=True)
        rstd = lax.rsqrt(jnp.mean(v * v, axis=-1, keepdims=True) + 1e-06)
        xhat = v * rstd
        dn = dn_ref[r]
        dx = dn * gain
        d = (
            dx
            - jnp.mean(dx, axis=-1, keepdims=True)
            - xhat * jnp.mean(dx * xhat, axis=-1, keepdims=True)
        ) * rstd
        out_ref[r] = d.astype(BF)
        for b in range(blocks):
            dd[b, r] = d[:, b * lanes : (b + 1) * lanes]
        g = cot_ref[r].astype(F32)
        acc[0] += fold(d)
        acc[1] += fold(dn * xhat)
        acc[2] += fold(dn)
        acc[3] += fold((g * layer).astype(BF).astype(F32))
        acc[4] += fold(g * (br_ref[r] + bias))
        return 0

    lax.fori_loop(0, rows, norm, 0)
    kk = KS * KS
    for t in range(5):
        small_ref[kk + t : kk + t + 1, :] = jnp.sum(acc[t], axis=0, keepdims=True) * scale
    n_pre = pre_ref.shape[0]
    small_ref[kk + 5 : kk + 5 + n_pre, :] = pre_ref[...] * scale
    left = small_ref.shape[0] - (kk + 5 + n_pre)
    if left:
        small_ref[kk + 5 + n_pre :, :] = jnp.zeros((left, chans), F32)

    part = 8

    def taps(b, _):
        at = pl.ds(pl.multiple_of(b * lanes, lanes), lanes)
        for j in range(KS):
            total = [jnp.zeros((8, lanes), F32) for _ in range(KS)]
            for p0 in range(0, rows, part):
                size = min(part, rows - p0)
                held = [dd[b, p0 + p] for p in range(size)]
                for r in range(size + KS - 1):
                    s = im[b, p0 + r, j : j + cols, :]
                    for i in range(KS):
                        if 0 <= r - i < size:
                            total[i] = total[i] + fold(held[r - i] * s)
            for i in range(KS):
                t = KS * i + j
                small_ref[t : t + 1, at] = jnp.sum(total[i], axis=0, keepdims=True) * scale
        return 0

    lax.fori_loop(0, blocks, taps, 0)


def backward(scale, padded, conv_out, d_normed, branch, cotangent, sum_pre, params):
    rows, cols, chans = conv_out.shape
    used = KS * KS + 5 + sum_pre.shape[0]
    total = -(-used // 32) * 32
    blocks = chans // 128
    return pl.pallas_call(
        functools.partial(backward_kernel, scale),
        out_shape=(
            jax.ShapeDtypeStruct((total, chans), F32),
            jax.ShapeDtypeStruct((rows, cols, chans), BF),
        ),
        scratch_shapes=[
            pltpu.VMEM((blocks, rows + KS - 1, cols + 8, 128), F32),
            pltpu.VMEM((blocks, rows, cols, 128), F32),
            pltpu.VMEM((8, 8, chans), F32),
        ],
        compiler_params=pltpu.CompilerParams(vmem_limit_bytes=16 * 1024 * 1024),
        cost_estimate=pl.CostEstimate(
            flops=2 * KS * KS * rows * cols * chans, bytes_accessed=8 * 1024 * 1024, transcendentals=0
        ),
        name="backward",
    )(padded, conv_out, d_normed, branch, cotangent, sum_pre, params)


def conv_kernel(ahead, pad_ref, w_ref, *refs):
    if ahead:
        par_ref, out_ref, normed_ref, im = refs
    else:
        start_ref, out_ref, im = refs
    rows, cols, chans = out_ref.shape
    high, wide, _ = pad_ref.shape
    lanes = 128
    blocks = chans // lanes
    kk = KS * KS

    def spread(r, _):
        row = pad_ref[r].astype(F32)
        for b in range(blocks):
            im[b, r, 0:wide, :] = row[:, b * lanes : (b + 1) * lanes]
        return 0

    lax.fori_loop(0, high, spread, 0)
    part = 8

    def block(b, _):
        at = pl.ds(pl.multiple_of(b * lanes, lanes), lanes)
        for p0 in range(0, rows, part):
            size = min(part, rows - p0)
            if ahead:
                acc = [jnp.zeros((cols, lanes), F32) + par_ref[0:1, at] for _ in range(size)]
            else:
                acc = [start_ref[p0 + p, :, at].astype(F32) for p in range(size)]
            for j in range(KS):
                spots = [KS * i + j for i in range(KS)]
                w = [
                    w_ref[t : t + 1, at] if ahead else w_ref[kk - 1 - t : kk - t, at]
                    for t in spots
                ]
                for r in range(size + KS - 1):
                    v = im[b, p0 + r, j : j + cols, :]
                    for i in range(KS):
                        if 0 <= r - i < size:
                            acc[r - i] = acc[r - i] + w[i] * v
            for p in range(size):
                out_ref[p0 + p, :, at] = acc[p]
        return 0

    lax.fori_loop(0, blocks, block, 0)
    if ahead:

        def norm(r, _):
            v = out_ref[r]
            v = v - jnp.mean(v, axis=-1, keepdims=True)
            rstd = lax.rsqrt(jnp.mean(v * v, axis=-1, keepdims=True) + 1e-06)
            normed_ref[r] = ((v * rstd) * par_ref[1:2, :] + par_ref[2:3, :]).astype(BF)
            return 0

        lax.fori_loop(0, rows, norm, 0)


def conv(ahead, padded, weights, extra):
    high, wide, chans = padded.shape
    shape = (high - KS + 1, wide - KS + 1, chans)
    out = jax.ShapeDtypeStruct(shape, F32)
    return pl.pallas_call(
        functools.partial(conv_kernel, ahead),
        out_shape=(out, jax.ShapeDtypeStruct(shape, BF)) if ahead else out,
        scratch_shapes=[pltpu.VMEM((chans // 128, high, shape[1] + 8, 128), F32)],
        compiler_params=pltpu.CompilerParams(vmem_limit_bytes=14 * 1024 * 1024),
        cost_estimate=pl.CostEstimate(
            flops=2 * KS * KS * math.prod(shape), bytes_accessed=16 * 1024 * 1024, transcendentals=0
        ),
        name="conv_norm" if ahead else "conv_image",
    )(padded, weights, extra)


def chunk_kernel(at_ref, pre_ref, hid_ref, normed_ref, db_ref, come_ref, *outs):
    unit = hid_ref.shape[1] // 16
    core = at_ref[0]
    me = (at_ref[1], at_ref[2])
    group = pl.program_id(0)
    first = core == 0
    lhs = jnp.where(first, pre_ref[...], hid_ref[...])
    rhs = jnp.where(first, normed_ref[...], db_ref[...])
    v = lax.dot_general(lhs, rhs, (((0,), (0,)), ((), ())), preferred_element_type=F32)
    v = v + come_ref[...].astype(F32)

    def store(k, row, value):
        value = value.astype(BF)
        rows = pl.ds(pl.multiple_of(row, 16), 2 * unit)
        for n in range(4):

            @pl.when(k == n)
            def _(n=n):
                outs[n][rows, :] = value

    def part(zh, x):
        t = zh * 4 + x
        return v[t * unit : (t + 1) * unit]

    @pl.when(first)
    def _():
        for x in range(4):
            k = lax.rem(x + 4 - me[0], 4)
            for zh in (0, 2):
                value = jnp.concatenate([part(zh, x), part(zh + 1, x)], axis=0)
                store(k, (group * 4 + zh) * unit, value)

    @pl.when(core == 1)
    def _():
        k = lax.rem(lax.rem(group, 4) + 4 - me[1], 4)
        for zh in range(4):
            for x in (0, 2):
                t = zh * 4 + x
                store(k, ((group // 4) * 16 + t) * unit, v[t * unit : (t + 2) * unit])


def chunks(d_pre, hidden, normed, d_branch, come):
    pixels, hid = hidden.shape
    chans = normed.shape[1]
    wide = hid // 8
    at = jnp.stack([lax.axis_index("c"), lax.axis_index("x"), lax.axis_index("y")]).astype(
        jnp.int32
    )
    whole = pl.BlockSpec((pixels, chans), lambda g: (0, 0))
    columns = pl.BlockSpec((pixels, wide), lambda g: (0, g))
    rows = hid // 4
    return pl.pallas_call(
        chunk_kernel,
        grid=(8,),
        in_specs=[
            pl.BlockSpec(memory_space=pltpu.SMEM),
            columns,
            columns,
            whole,
            whole,
            pl.BlockSpec((wide, chans), lambda g: (g, 0)),
        ],
        out_specs=[pl.BlockSpec((rows, chans), lambda g: (0, 0))] * 4,
        out_shape=[pltpu.HBM((rows, chans), BF)] * 4,
        compiler_params=pltpu.CompilerParams(vmem_limit_bytes=22 * 1024 * 1024),
        cost_estimate=pl.CostEstimate(
            flops=2 * pixels * hid * chans, bytes_accessed=18 * 1024 * 1024, transcendentals=0
        ),
        name="chunks",
    )(at, d_pre, hidden, normed, d_branch, come)


def on_device(
    image,
    conv_weight,
    conv_bias,
    layernorm_gain,
    layernorm_bias,
    w_expand,
    b_expand,
    w_reduce,
    b_reduce,
    layer_scale,
    cotangent,
):
    rows, cols, chans = image.shape
    hid = w_expand.shape[0]
    per = hid // 256
    scale = 1.0 / math.sqrt(rows * cols * 256)
    first = lax.axis_index("c") == 0
    padded = halo_rows(halo_columns(image, 3), 3)
    kernel = conv_weight.reshape(KS * KS, chans)
    conv_out, normed = conv(
        True,
        padded,
        kernel,
        jnp.stack([conv_bias, layernorm_gain, layernorm_bias] + [layernorm_bias] * 5),
    )
    normed = normed.reshape(rows * cols, chans)
    pre = (
        lax.dot_general(normed, w_expand, (((1,), (1,)), ((), ())), preferred_element_type=F32)
        + b_expand
    )
    act, slope = gelu_pair(pre)
    hidden = act.astype(BF)
    grad_f = cotangent.reshape(rows * cols, chans).astype(F32)
    d_branch = (layer_scale * grad_f).astype(BF)
    d_hidden = jnp.dot(d_branch, w_reduce, preferred_element_type=F32)
    d_pre = (d_hidden * slope).astype(BF)

    far = tdot(jnp.where(first, hidden, d_pre), jnp.where(first, d_branch, normed)).astype(BF)
    come = core_swap(far)
    branch = lax.dot_general(
        hidden, w_reduce, (((1,), (1,)), ((), ())), preferred_element_type=F32
    )
    d_normed = jnp.dot(d_pre, w_expand, preferred_element_type=F32)
    sum_pre = jnp.sum(d_pre.astype(F32), axis=0).reshape(hid // chans, chans)
    params = jnp.stack([layernorm_gain, b_reduce, layer_scale] + [layer_scale] * 5)
    shape = (rows, cols, chans)

    moved = list(chunks(d_pre, hidden, normed, d_branch, come))
    got = split_move(moved, ("x", "y"))
    d_normed, moved[0] = lax.optimization_barrier((d_normed, moved[0]))
    small, d_conv = backward(
        scale,
        padded,
        conv_out,
        d_normed.reshape(shape),
        branch.reshape(shape),
        cotangent,
        sum_pre,
        params,
    )
    total = small.shape[0]
    lower, upper = small[: total // 2], small[total // 2 :]
    small = jnp.where(first, lower, upper) + core_swap(jnp.where(first, upper, lower))
    low = small.astype(BF)
    small = low.astype(F32) + zl_swap(low).astype(F32)
    wide = halo_columns(d_conv, 3)
    d_pad = halo_rows(wide, 3)
    got, small, wide = lax.optimization_barrier((got, small, wide))
    term = add_all([moved[0]] + got).astype(BF).reshape(2, 4, 4, 2 * per, chans)

    moved = split_send(term, small, ("y", "x"), (1, 2))
    got = split_move(moved, ("y", "x"))
    term, small = split_add(moved, got, small.shape[0])
    term = term.astype(BF).reshape(2, 4, 2 * per, chans)
    d_pad, _ = lax.optimization_barrier((d_pad, term))
    grad_image = conv(False, d_pad, kernel, cotangent)
    term, small, grad_image = z_sum(term, small, grad_image)
    term = term * scale
    top, low = term[:per], term[per:]
    got = core_swap(jnp.concatenate([small, jnp.where(first, low, top)], axis=0))
    keep = jnp.where(first, top, low)
    other, got = got[: total // 2], got[total // 2 :]
    small = jnp.concatenate(
        [jnp.where(first, small, other), jnp.where(first, other, small)], axis=0
    )
    grad_expand = jnp.where(first, keep, got)
    grad_reduce = jnp.where(first, got, keep).T

    kk = KS * KS
    return (
        grad_image,
        grad_expand,
        grad_reduce,
        small[:kk].reshape(KS, KS, chans),
        small[kk],
        small[kk + 1],
        small[kk + 2],
        small[kk + 5 : kk + 5 + hid // chans].reshape(hid),
        small[kk + 3],
        small[kk + 4],
    )


def solution(mesh):
    grid = Mesh(mesh.devices.reshape(SIZES), AXES)
    tile = P(ROW, COL, None)
    one = P()
    in_specs = (tile,) + (one,) * 9 + (tile,)
    out_specs = (tile, P(AXES, None), P(None, AXES)) + (one,) * 7
    return jax.shard_map(
        on_device, mesh=grid, in_specs=in_specs, out_specs=out_specs, check_vma=False
    )
```

```python
import functools
import itertools
import math

import jax
import jax.numpy as jnp
from jax import lax
from jax.experimental import pallas as pl
from jax.experimental.pallas import tpu as pltpu
from jax.sharding import Mesh
from jax.sharding import PartitionSpec as P

KS = 7
AXES = ("zl", "y", "zh", "x", "c")
SIZES = (2, 4, 4, 4, 2)
ROW = ("zl", "y")
COL = ("zh", "x", "c")
BF = jnp.bfloat16
F32 = jnp.float32


def core_pairs(k, lead):
    pairs = []
    for spot in itertools.product(*(range(n) for n in SIZES)):
        to = list(spot)
        at = AXES.index(lead[spot[-1]])
        to[at] = (to[at] + k) % SIZES[at]
        pairs.append((flat_index(spot), flat_index(to)))
    return pairs


def flat_index(spot):
    out = 0
    for i, n in zip(spot, SIZES):
        out = out * n + i
    return out


def split_send(v, small, lead, dims):
    core = lax.axis_index("c")
    me = [lax.axis_index(name) for name in lead]
    chans = v.shape[-1]

    def pick(k):
        parts = [
            lax.dynamic_index_in_dim(v, lax.rem(me[s] + k, 4), dims[s], keepdims=False).reshape(
                -1, chans
            )
            for s in range(2)
        ]
        return jnp.where(core == 0, parts[0], parts[1])

    low = small.astype(BF)
    return [jnp.concatenate([low, pick(k)], axis=0) for k in range(4)]


def split_move(moved, lead):
    return [lax.ppermute(moved[k], AXES, core_pairs(k, lead)) for k in range(1, 4)]


def split_add(moved, got, count):
    def add(part):
        out = part(moved[0]).astype(F32)
        for v in got:
            out = out + part(v).astype(F32)
        return out

    return add(lambda v: v[count:]), add(lambda v: v[:count])


def add_all(parts):
    out = parts[0].astype(F32)
    for v in parts[1:]:
        out = out + v.astype(F32)
    return out


def z_sum(v, small, work):
    count, chans = small.shape
    zl = lax.axis_index("zl")
    zh = lax.axis_index("zh")
    away = lax.dynamic_index_in_dim(v, 1 - zl, 0, False).reshape(-1, chans)
    near = lax.dynamic_index_in_dim(v, zl, 0, False).reshape(-1, chans)
    low = small.astype(BF)
    got = zl_swap(away)
    others = split_move([low] * 4, ("x", "y"))
    low = add_all([low] + others).astype(BF)
    v = (near.astype(F32) + got.astype(F32)).astype(BF).reshape(v.shape[1:])
    kept = jnp.concatenate([low, lax.dynamic_index_in_dim(v, zh, 0, False)], axis=0)
    back = []
    for k in range(1, 4):
        part = lax.dynamic_index_in_dim(v, lax.rem(zh + k, 4), 0, False)
        sent = jnp.concatenate([low, part], axis=0)
        back.append(lax.ppermute(sent, "zh", [(i, (i + k) % 4) for i in range(4)]))
    beside = work(v)
    back, beside = lax.optimization_barrier((back, beside))
    acc, sums = split_add([kept], back, count)
    return acc, sums, beside


def zl_swap(v):
    return lax.ppermute(v, "zl", [(0, 1), (1, 0)])


def core_swap(v):
    return lax.ppermute(v, "c", [(0, 1), (1, 0)])


def shift(v, axes, d):
    n = lax.axis_size(axes)
    return lax.ppermute(v, axes, [(i, i + d) for i in range(n) if 0 <= i + d < n])


def halo_columns(x, w):
    west = shift(x[:, x.shape[1] - w :], COL, 1)
    east = shift(x[:, :w], COL, -1)
    return jnp.concatenate([west, x, east], axis=1)


def halo_rows(x, w):
    north = shift(x[x.shape[0] - w :], ROW, 1)
    south = shift(x[:w], ROW, -1)
    return jnp.concatenate([north, x, south], axis=0)


def gelu_pair(pre):
    root = pre / math.sqrt(2.0)
    cdf = 0.5 * (1.0 + lax.erf(root))
    return (pre * cdf, cdf + pre * jnp.exp(-0.5 * pre * pre) / math.sqrt(2.0 * math.pi))


def tdot(a, b):
    return lax.dot_general(a, b, (((0,), (0,)), ((), ())), preferred_element_type=F32)


def backward_kernel(
    scale, pad_ref, conv_ref, dn_ref, br_ref, cot_ref, pre_ref, par_ref, small_ref, out_ref, im, dd, acc
):
    rows, cols, chans = conv_ref.shape
    lanes = 128
    blocks = chans // lanes
    high, wide, _ = pad_ref.shape
    gain = par_ref[0:1, :]
    bias = par_ref[1:2, :]
    layer = par_ref[2:3, :]
    acc[...] = jnp.zeros_like(acc)

    def spread(r, _):
        row = pad_ref[r].astype(F32)
        for b in range(blocks):
            im[b, r, 0:wide, :] = row[:, b * lanes : (b + 1) * lanes]
        return 0

    lax.fori_loop(0, high, spread, 0)

    def fold(v):
        out = v[0:8]
        for t in range(8, cols, 8):
            out = out + v[t : t + 8]
        return out

    def norm(r, _):
        v = conv_ref[r]
        v = v - jnp.mean(v, axis=-1, keepdims=True)
        rstd = lax.rsqrt(jnp.mean(v * v, axis=-1, keepdims=True) + 1e-06)
        xhat = v * rstd
        dn = dn_ref[r]
        dx = dn * gain
        d = (
            dx
            - jnp.mean(dx, axis=-1, keepdims=True)
            - xhat * jnp.mean(dx * xhat, axis=-1, keepdims=True)
        ) * rstd
        out_ref[r] = d.astype(BF)
        for b in range(blocks):
            dd[b, r] = d[:, b * lanes : (b + 1) * lanes]
        g = cot_ref[r].astype(F32)
        acc[0] += fold(d)
        acc[1] += fold(dn * xhat)
        acc[2] += fold(dn)
        acc[3] += fold((g * layer).astype(BF).astype(F32))
        acc[4] += fold(g * (br_ref[r] + bias))
        return 0

    lax.fori_loop(0, rows, norm, 0)
    kk = KS * KS
    for t in range(5):
        small_ref[kk + t : kk + t + 1, :] = jnp.sum(acc[t], axis=0, keepdims=True) * scale
    n_pre = pre_ref.shape[0]
    small_ref[kk + 5 : kk + 5 + n_pre, :] = pre_ref[...] * scale
    left = small_ref.shape[0] - (kk + 5 + n_pre)
    if left:
        small_ref[kk + 5 + n_pre :, :] = jnp.zeros((left, chans), F32)

    part = 8

    def taps(b, _):
        at = pl.ds(pl.multiple_of(b * lanes, lanes), lanes)
        for j in range(KS):
            total = [jnp.zeros((8, lanes), F32) for _ in range(KS)]
            for p0 in range(0, rows, part):
                size = min(part, rows - p0)
                held = [dd[b, p0 + p] for p in range(size)]
                for r in range(size + KS - 1):
                    s = im[b, p0 + r, j : j + cols, :]
                    for i in range(KS):
                        if 0 <= r - i < size:
                            total[i] = total[i] + fold(held[r - i] * s)
            for i in range(KS):
                t = KS * i + j
                small_ref[t : t + 1, at] = jnp.sum(total[i], axis=0, keepdims=True) * scale
        return 0

    lax.fori_loop(0, blocks, taps, 0)


def backward(scale, padded, conv_out, d_normed, branch, cotangent, sum_pre, params):
    rows, cols, chans = conv_out.shape
    used = KS * KS + 5 + sum_pre.shape[0]
    total = -(-used // 32) * 32
    blocks = chans // 128
    return pl.pallas_call(
        functools.partial(backward_kernel, scale),
        out_shape=(
            jax.ShapeDtypeStruct((total, chans), F32),
            jax.ShapeDtypeStruct((rows, cols, chans), BF),
        ),
        scratch_shapes=[
            pltpu.VMEM((blocks, rows + KS - 1, cols + 8, 128), F32),
            pltpu.VMEM((blocks, rows, cols, 128), F32),
            pltpu.VMEM((8, 8, chans), F32),
        ],
        compiler_params=pltpu.CompilerParams(vmem_limit_bytes=16 * 1024 * 1024),
        cost_estimate=pl.CostEstimate(
            flops=2 * KS * KS * rows * cols * chans, bytes_accessed=8 * 1024 * 1024, transcendentals=0
        ),
        name="backward",
    )(padded, conv_out, d_normed, branch, cotangent, sum_pre, params)


def conv_kernel(ahead, pad_ref, w_ref, *refs):
    if ahead:
        par_ref, out_ref, normed_ref, im = refs
    else:
        start_ref, out_ref, im = refs
    rows, cols, chans = out_ref.shape
    high, wide, _ = pad_ref.shape
    lanes = 128
    blocks = chans // lanes
    kk = KS * KS

    def spread(r, _):
        row = pad_ref[r].astype(F32)
        for b in range(blocks):
            im[b, r, 0:wide, :] = row[:, b * lanes : (b + 1) * lanes]
        return 0

    lax.fori_loop(0, high, spread, 0)
    part = 8

    def block(b, _):
        at = pl.ds(pl.multiple_of(b * lanes, lanes), lanes)
        for p0 in range(0, rows, part):
            size = min(part, rows - p0)
            if ahead:
                acc = [jnp.zeros((cols, lanes), F32) + par_ref[0:1, at] for _ in range(size)]
            else:
                acc = [start_ref[p0 + p, :, at].astype(F32) for p in range(size)]
            for j in range(KS):
                spots = [KS * i + j for i in range(KS)]
                w = [
                    w_ref[t : t + 1, at] if ahead else w_ref[kk - 1 - t : kk - t, at]
                    for t in spots
                ]
                for r in range(size + KS - 1):
                    v = im[b, p0 + r, j : j + cols, :]
                    for i in range(KS):
                        if 0 <= r - i < size:
                            acc[r - i] = acc[r - i] + w[i] * v
            for p in range(size):
                out_ref[p0 + p, :, at] = acc[p]
        return 0

    lax.fori_loop(0, blocks, block, 0)
    if ahead:

        def norm(r, _):
            v = out_ref[r]
            v = v - jnp.mean(v, axis=-1, keepdims=True)
            rstd = lax.rsqrt(jnp.mean(v * v, axis=-1, keepdims=True) + 1e-06)
            normed_ref[r] = ((v * rstd) * par_ref[1:2, :] + par_ref[2:3, :]).astype(BF)
            return 0

        lax.fori_loop(0, rows, norm, 0)


def conv(ahead, padded, weights, extra):
    high, wide, chans = padded.shape
    shape = (high - KS + 1, wide - KS + 1, chans)
    out = jax.ShapeDtypeStruct(shape, F32)
    return pl.pallas_call(
        functools.partial(conv_kernel, ahead),
        out_shape=(out, jax.ShapeDtypeStruct(shape, BF)) if ahead else out,
        scratch_shapes=[pltpu.VMEM((chans // 128, high, shape[1] + 8, 128), F32)],
        compiler_params=pltpu.CompilerParams(vmem_limit_bytes=14 * 1024 * 1024),
        cost_estimate=pl.CostEstimate(
            flops=2 * KS * KS * math.prod(shape), bytes_accessed=16 * 1024 * 1024, transcendentals=0
        ),
        name="conv_norm" if ahead else "conv_image",
    )(padded, weights, extra)


def chunk_kernel(at_ref, pre_ref, hid_ref, normed_ref, db_ref, come_ref, *rest):
    outs, held, sems = rest[:4], rest[4], rest[5]
    unit = hid_ref.shape[1] // 16
    core = at_ref[0]
    me = (at_ref[1], at_ref[2])
    group = pl.program_id(0)
    first = core == 0
    lhs = jnp.where(first, pre_ref[...], hid_ref[...])
    rhs = jnp.where(first, normed_ref[...], db_ref[...])
    v = lax.dot_general(lhs, rhs, (((0,), (0,)), ((), ())), preferred_element_type=F32)
    v = v + come_ref[...].astype(F32)

    def store(k, row, value):
        held[k, pl.ds(pl.multiple_of(row, 16), 2 * unit), :] = value.astype(BF)

    def part(zh, x):
        t = zh * 4 + x
        return v[t * unit : (t + 1) * unit]

    @pl.when(first)
    def _():
        for x in range(4):
            k = lax.rem(x + 4 - me[0], 4)
            for zh in (0, 2):
                value = jnp.concatenate([part(zh, x), part(zh + 1, x)], axis=0)
                store(k, (group * 4 + zh) * unit, value)

    @pl.when(core == 1)
    def _():
        k = lax.rem(lax.rem(group, 4) + 4 - me[1], 4)
        for zh in range(4):
            for x in (0, 2):
                t = zh * 4 + x
                store(k, ((group // 4) * 16 + t) * unit, v[t * unit : (t + 2) * unit])

    @pl.when(group == pl.num_programs(0) - 1)
    def _():
        copies = [pltpu.make_async_copy(held.at[n], outs[n], sems.at[n]) for n in range(4)]
        for copy in copies:
            copy.start()
        for copy in copies:
            copy.wait()


def chunks(d_pre, hidden, normed, d_branch, come):
    pixels, hid = hidden.shape
    chans = normed.shape[1]
    wide = hid // 8
    at = jnp.stack([lax.axis_index("c"), lax.axis_index("x"), lax.axis_index("y")]).astype(
        jnp.int32
    )
    whole = pl.BlockSpec((pixels, chans), lambda g: (0, 0))
    columns = pl.BlockSpec((pixels, wide), lambda g: (0, g))
    rows = hid // 4
    return pl.pallas_call(
        chunk_kernel,
        grid=(8,),
        in_specs=[
            pl.BlockSpec(memory_space=pltpu.SMEM),
            columns,
            columns,
            whole,
            whole,
            pl.BlockSpec((wide, chans), lambda g: (g, 0)),
        ],
        out_specs=[pl.BlockSpec(memory_space=pl.ANY)] * 4,
        out_shape=[pltpu.HBM((rows, chans), BF)] * 4,
        scratch_shapes=[pltpu.VMEM((4, rows, chans), BF), pltpu.SemaphoreType.DMA((4,))],
        compiler_params=pltpu.CompilerParams(vmem_limit_bytes=22 * 1024 * 1024),
        cost_estimate=pl.CostEstimate(
            flops=2 * pixels * hid * chans, bytes_accessed=18 * 1024 * 1024, transcendentals=0
        ),
        name="chunks",
    )(at, d_pre, hidden, normed, d_branch, come)


def on_device(
    image,
    conv_weight,
    conv_bias,
    layernorm_gain,
    layernorm_bias,
    w_expand,
    b_expand,
    w_reduce,
    b_reduce,
    layer_scale,
    cotangent,
):
    rows, cols, chans = image.shape
    hid = w_expand.shape[0]
    per = hid // 256
    scale = 1.0 / math.sqrt(rows * cols * 256)
    first = lax.axis_index("c") == 0
    padded = halo_rows(halo_columns(image, 3), 3)
    kernel = conv_weight.reshape(KS * KS, chans)
    conv_out, normed = conv(
        True,
        padded,
        kernel,
        jnp.stack([conv_bias, layernorm_gain, layernorm_bias] + [layernorm_bias] * 5),
    )
    normed = normed.reshape(rows * cols, chans)
    pre = (
        lax.dot_general(normed, w_expand, (((1,), (1,)), ((), ())), preferred_element_type=F32)
        + b_expand
    )
    act, slope = gelu_pair(pre)
    hidden = act.astype(BF)
    grad_f = cotangent.reshape(rows * cols, chans).astype(F32)
    d_branch = (layer_scale * grad_f).astype(BF)
    d_hidden = jnp.dot(d_branch, w_reduce, preferred_element_type=F32)
    d_pre = (d_hidden * slope).astype(BF)

    far = tdot(jnp.where(first, hidden, d_pre), jnp.where(first, d_branch, normed)).astype(BF)
    come = core_swap(far)
    branch = lax.dot_general(
        hidden, w_reduce, (((1,), (1,)), ((), ())), preferred_element_type=F32
    )
    d_normed = jnp.dot(d_pre, w_expand, preferred_element_type=F32)
    sum_pre = jnp.sum(d_pre.astype(F32), axis=0).reshape(hid // chans, chans)
    params = jnp.stack([layernorm_gain, b_reduce, layer_scale] + [layer_scale] * 5)
    shape = (rows, cols, chans)

    moved = list(chunks(d_pre, hidden, normed, d_branch, come))
    got = split_move(moved, ("x", "y"))
    d_normed, moved[0] = lax.optimization_barrier((d_normed, moved[0]))
    small, d_conv = backward(
        scale,
        padded,
        conv_out,
        d_normed.reshape(shape),
        branch.reshape(shape),
        cotangent,
        sum_pre,
        params,
    )
    total = small.shape[0]
    lower, upper = small[: total // 2], small[total // 2 :]
    small = jnp.where(first, lower, upper) + core_swap(jnp.where(first, upper, lower))
    low = small.astype(BF)
    small = low.astype(F32) + zl_swap(low).astype(F32)
    wide = halo_columns(d_conv, 3)
    d_pad = halo_rows(wide, 3)
    got, small, wide = lax.optimization_barrier((got, small, wide))
    term = add_all([moved[0]] + got).astype(BF).reshape(2, 4, 4, 2 * per, chans)

    moved = split_send(term, small, ("y", "x"), (1, 2))
    got = split_move(moved, ("y", "x"))
    term, small = split_add(moved, got, small.shape[0])
    term = term.astype(BF).reshape(2, 4, 2 * per, chans)

    def image_part(after):
        return conv(False, lax.optimization_barrier((d_pad, after))[0], kernel, cotangent)

    term, small, grad_image = z_sum(term, small, image_part)
    term = term * scale
    top, low = term[:per], term[per:]
    got = core_swap(jnp.concatenate([small, jnp.where(first, low, top)], axis=0))
    keep = jnp.where(first, top, low)
    other, got = got[: total // 2], got[total // 2 :]
    small = jnp.concatenate(
        [jnp.where(first, small, other), jnp.where(first, other, small)], axis=0
    )
    grad_expand = jnp.where(first, keep, got)
    grad_reduce = jnp.where(first, got, keep).T

    kk = KS * KS
    return (
        grad_image,
        grad_expand,
        grad_reduce,
        small[:kk].reshape(KS, KS, chans),
        small[kk],
        small[kk + 1],
        small[kk + 2],
        small[kk + 5 : kk + 5 + hid // chans].reshape(hid),
        small[kk + 3],
        small[kk + 4],
    )


def solution(mesh):
    grid = Mesh(mesh.devices.reshape(SIZES), AXES)
    tile = P(ROW, COL, None)
    one = P()
    in_specs = (tile,) + (one,) * 9 + (tile,)
    out_specs = (tile, P(AXES, None), P(None, AXES)) + (one,) * 7
    return jax.shard_map(
        on_device, mesh=grid, in_specs=in_specs, out_specs=out_specs, check_vma=False
    )
```

```python
import functools
import itertools
import math

import jax
import jax.numpy as jnp
from jax import lax
from jax.experimental import pallas as pl
from jax.experimental.pallas import tpu as pltpu
from jax.sharding import Mesh
from jax.sharding import PartitionSpec as P

KS = 7
AXES = ("zl", "y", "zh", "x", "c")
SIZES = (2, 4, 4, 4, 2)
ROW = ("zl", "y")
COL = ("zh", "x", "c")
BF = jnp.bfloat16
F32 = jnp.float32


def core_pairs(k, lead):
    pairs = []
    for spot in itertools.product(*(range(n) for n in SIZES)):
        to = list(spot)
        at = AXES.index(lead[spot[-1]])
        to[at] = (to[at] + k) % SIZES[at]
        pairs.append((flat_index(spot), flat_index(to)))
    return pairs


def flat_index(spot):
    out = 0
    for i, n in zip(spot, SIZES):
        out = out * n + i
    return out


def split_send(v, small, lead, dims):
    core = lax.axis_index("c")
    me = [lax.axis_index(name) for name in lead]
    chans = v.shape[-1]

    def pick(k):
        parts = [
            lax.dynamic_index_in_dim(v, lax.rem(me[s] + k, 4), dims[s], keepdims=False).reshape(
                -1, chans
            )
            for s in range(2)
        ]
        return jnp.where(core == 0, parts[0], parts[1])

    low = small.astype(BF)
    return [jnp.concatenate([low, pick(k)], axis=0) for k in range(4)]


def split_move(moved, lead):
    return [lax.ppermute(moved[k], AXES, core_pairs(k, lead)) for k in range(1, 4)]


def split_add(moved, got, count):
    def add(part):
        out = part(moved[0]).astype(F32)
        for v in got:
            out = out + part(v).astype(F32)
        return out

    return add(lambda v: v[count:]), add(lambda v: v[:count])


def add_all(parts):
    out = parts[0].astype(F32)
    for v in parts[1:]:
        out = out + v.astype(F32)
    return out


def z_sum(v, small, work):
    count, chans = small.shape
    v, small = lax.optimization_barrier((v, small))
    zl = lax.axis_index("zl")
    zh = lax.axis_index("zh")
    away = lax.dynamic_index_in_dim(v, 1 - zl, 0, False).reshape(-1, chans)
    near = lax.dynamic_index_in_dim(v, zl, 0, False).reshape(-1, chans)
    low = small.astype(BF)
    got = zl_swap(away)
    others = split_move([low] * 4, ("x", "y"))
    low = add_all([low] + others).astype(BF)
    v = (near.astype(F32) + got.astype(F32)).astype(BF).reshape(v.shape[1:])
    kept = jnp.concatenate([low, lax.dynamic_index_in_dim(v, zh, 0, False)], axis=0)
    back = []
    for k in range(1, 4):
        part = lax.dynamic_index_in_dim(v, lax.rem(zh + k, 4), 0, False)
        sent = jnp.concatenate([low, part], axis=0)
        back.append(lax.ppermute(sent, "zh", [(i, (i + k) % 4) for i in range(4)]))
    beside = work(v)
    back, beside = lax.optimization_barrier((back, beside))
    acc, sums = split_add([kept], back, count)
    return acc, sums, beside


def zl_swap(v):
    return lax.ppermute(v, "zl", [(0, 1), (1, 0)])


def core_swap(v):
    return lax.ppermute(v, "c", [(0, 1), (1, 0)])


def shift(v, axes, d):
    n = lax.axis_size(axes)
    return lax.ppermute(v, axes, [(i, i + d) for i in range(n) if 0 <= i + d < n])


def halo_columns(x, w):
    west = shift(x[:, x.shape[1] - w :], COL, 1)
    east = shift(x[:, :w], COL, -1)
    return jnp.concatenate([west, x, east], axis=1)


def halo_rows(x, w):
    north = shift(x[x.shape[0] - w :], ROW, 1)
    south = shift(x[:w], ROW, -1)
    return jnp.concatenate([north, x, south], axis=0)


def gelu_pair(pre):
    root = pre / math.sqrt(2.0)
    cdf = 0.5 * (1.0 + lax.erf(root))
    return (pre * cdf, cdf + pre * jnp.exp(-0.5 * pre * pre) / math.sqrt(2.0 * math.pi))


def tdot(a, b):
    return lax.dot_general(a, b, (((0,), (0,)), ((), ())), preferred_element_type=F32)


def backward_kernel(
    scale, pad_ref, conv_ref, dn_ref, br_ref, cot_ref, pre_ref, par_ref, small_ref, out_ref, im, dd, acc
):
    rows, cols, chans = conv_ref.shape
    lanes = 128
    blocks = chans // lanes
    high, wide, _ = pad_ref.shape
    gain = par_ref[0:1, :]
    bias = par_ref[1:2, :]
    layer = par_ref[2:3, :]
    acc[...] = jnp.zeros_like(acc)

    def spread(r, _):
        row = pad_ref[r].astype(F32)
        for b in range(blocks):
            im[b, r, 0:wide, :] = row[:, b * lanes : (b + 1) * lanes]
        return 0

    lax.fori_loop(0, high, spread, 0)

    def fold(v):
        out = v[0:8]
        for t in range(8, cols, 8):
            out = out + v[t : t + 8]
        return out

    def norm(r, _):
        v = conv_ref[r]
        v = v - jnp.mean(v, axis=-1, keepdims=True)
        rstd = lax.rsqrt(jnp.mean(v * v, axis=-1, keepdims=True) + 1e-06)
        xhat = v * rstd
        dn = dn_ref[r]
        dx = dn * gain
        d = (
            dx
            - jnp.mean(dx, axis=-1, keepdims=True)
            - xhat * jnp.mean(dx * xhat, axis=-1, keepdims=True)
        ) * rstd
        out_ref[r] = d.astype(BF)
        for b in range(blocks):
            dd[b, r] = d[:, b * lanes : (b + 1) * lanes]
        g = cot_ref[r].astype(F32)
        acc[0] += fold(d)
        acc[1] += fold(dn * xhat)
        acc[2] += fold(dn)
        acc[3] += fold((g * layer).astype(BF).astype(F32))
        acc[4] += fold(g * (br_ref[r] + bias))
        return 0

    lax.fori_loop(0, rows, norm, 0)
    kk = KS * KS
    for t in range(5):
        small_ref[kk + t : kk + t + 1, :] = jnp.sum(acc[t], axis=0, keepdims=True) * scale
    n_pre = pre_ref.shape[0]
    small_ref[kk + 5 : kk + 5 + n_pre, :] = pre_ref[...] * scale
    left = small_ref.shape[0] - (kk + 5 + n_pre)
    if left:
        small_ref[kk + 5 + n_pre :, :] = jnp.zeros((left, chans), F32)

    part = 8

    def taps(b, _):
        at = pl.ds(pl.multiple_of(b * lanes, lanes), lanes)
        for j in range(KS):
            total = [jnp.zeros((8, lanes), F32) for _ in range(KS)]
            for p0 in range(0, rows, part):
                size = min(part, rows - p0)
                held = [dd[b, p0 + p] for p in range(size)]
                for r in range(size + KS - 1):
                    s = im[b, p0 + r, j : j + cols, :]
                    for i in range(KS):
                        if 0 <= r - i < size:
                            total[i] = total[i] + fold(held[r - i] * s)
            for i in range(KS):
                t = KS * i + j
                small_ref[t : t + 1, at] = jnp.sum(total[i], axis=0, keepdims=True) * scale
        return 0

    lax.fori_loop(0, blocks, taps, 0)


def backward(scale, padded, conv_out, d_normed, branch, cotangent, sum_pre, params):
    rows, cols, chans = conv_out.shape
    used = KS * KS + 5 + sum_pre.shape[0]
    total = -(-used // 32) * 32
    blocks = chans // 128
    return pl.pallas_call(
        functools.partial(backward_kernel, scale),
        out_shape=(
            jax.ShapeDtypeStruct((total, chans), F32),
            jax.ShapeDtypeStruct((rows, cols, chans), BF),
        ),
        scratch_shapes=[
            pltpu.VMEM((blocks, rows + KS - 1, cols + 8, 128), F32),
            pltpu.VMEM((blocks, rows, cols, 128), F32),
            pltpu.VMEM((8, 8, chans), F32),
        ],
        compiler_params=pltpu.CompilerParams(vmem_limit_bytes=16 * 1024 * 1024),
        cost_estimate=pl.CostEstimate(
            flops=2 * KS * KS * rows * cols * chans, bytes_accessed=8 * 1024 * 1024, transcendentals=0
        ),
        name="backward",
    )(padded, conv_out, d_normed, branch, cotangent, sum_pre, params)


def conv_kernel(ahead, pad_ref, w_ref, *refs):
    if ahead:
        par_ref, out_ref, normed_ref, im = refs
    else:
        start_ref, out_ref, im = refs
    rows, cols, chans = out_ref.shape
    high, wide, _ = pad_ref.shape
    lanes = 128
    blocks = chans // lanes
    kk = KS * KS

    def spread(r, _):
        row = pad_ref[r].astype(F32)
        for b in range(blocks):
            im[b, r, 0:wide, :] = row[:, b * lanes : (b + 1) * lanes]
        return 0

    lax.fori_loop(0, high, spread, 0)
    part = 8

    def block(b, _):
        at = pl.ds(pl.multiple_of(b * lanes, lanes), lanes)
        for p0 in range(0, rows, part):
            size = min(part, rows - p0)
            if ahead:
                acc = [jnp.zeros((cols, lanes), F32) + par_ref[0:1, at] for _ in range(size)]
            else:
                acc = [start_ref[p0 + p, :, at].astype(F32) for p in range(size)]
            for j in range(KS):
                spots = [KS * i + j for i in range(KS)]
                w = [
                    w_ref[t : t + 1, at] if ahead else w_ref[kk - 1 - t : kk - t, at]
                    for t in spots
                ]
                for r in range(size + KS - 1):
                    v = im[b, p0 + r, j : j + cols, :]
                    for i in range(KS):
                        if 0 <= r - i < size:
                            acc[r - i] = acc[r - i] + w[i] * v
            for p in range(size):
                out_ref[p0 + p, :, at] = acc[p]
        return 0

    lax.fori_loop(0, blocks, block, 0)
    if ahead:

        def norm(r, _):
            v = out_ref[r]
            v = v - jnp.mean(v, axis=-1, keepdims=True)
            rstd = lax.rsqrt(jnp.mean(v * v, axis=-1, keepdims=True) + 1e-06)
            normed_ref[r] = ((v * rstd) * par_ref[1:2, :] + par_ref[2:3, :]).astype(BF)
            return 0

        lax.fori_loop(0, rows, norm, 0)


def conv(ahead, padded, weights, extra):
    high, wide, chans = padded.shape
    shape = (high - KS + 1, wide - KS + 1, chans)
    out = jax.ShapeDtypeStruct(shape, F32)
    return pl.pallas_call(
        functools.partial(conv_kernel, ahead),
        out_shape=(out, jax.ShapeDtypeStruct(shape, BF)) if ahead else out,
        scratch_shapes=[pltpu.VMEM((chans // 128, high, shape[1] + 8, 128), F32)],
        compiler_params=pltpu.CompilerParams(vmem_limit_bytes=14 * 1024 * 1024),
        cost_estimate=pl.CostEstimate(
            flops=2 * KS * KS * math.prod(shape), bytes_accessed=16 * 1024 * 1024, transcendentals=0
        ),
        name="conv_norm" if ahead else "conv_image",
    )(padded, weights, extra)


def chunk_kernel(at_ref, pre_ref, hid_ref, normed_ref, db_ref, come_ref, *rest):
    outs, held, sems = rest[:4], rest[4], rest[5]
    unit = hid_ref.shape[1] // 16
    core = at_ref[0]
    me = (at_ref[1], at_ref[2])
    group = pl.program_id(0)
    first = core == 0
    lhs = jnp.where(first, pre_ref[...], hid_ref[...])
    rhs = jnp.where(first, normed_ref[...], db_ref[...])
    v = lax.dot_general(lhs, rhs, (((0,), (0,)), ((), ())), preferred_element_type=F32)
    v = v + come_ref[...].astype(F32)

    def store(k, row, value):
        held[k, pl.ds(pl.multiple_of(row, 16), 2 * unit), :] = value.astype(BF)

    def part(zh, x):
        t = zh * 4 + x
        return v[t * unit : (t + 1) * unit]

    @pl.when(first)
    def _():
        for x in range(4):
            k = lax.rem(x + 4 - me[0], 4)
            for zh in (0, 2):
                value = jnp.concatenate([part(zh, x), part(zh + 1, x)], axis=0)
                store(k, (group * 4 + zh) * unit, value)

    @pl.when(core == 1)
    def _():
        k = lax.rem(lax.rem(group, 4) + 4 - me[1], 4)
        for zh in range(4):
            for x in (0, 2):
                t = zh * 4 + x
                store(k, ((group // 4) * 16 + t) * unit, v[t * unit : (t + 2) * unit])

    @pl.when(group == pl.num_programs(0) - 1)
    def _():
        copies = [pltpu.make_async_copy(held.at[n], outs[n], sems.at[n]) for n in range(4)]
        for copy in copies:
            copy.start()
        for copy in copies:
            copy.wait()


def chunks(d_pre, hidden, normed, d_branch, come):
    pixels, hid = hidden.shape
    chans = normed.shape[1]
    wide = hid // 8
    at = jnp.stack([lax.axis_index("c"), lax.axis_index("x"), lax.axis_index("y")]).astype(
        jnp.int32
    )
    whole = pl.BlockSpec((pixels, chans), lambda g: (0, 0))
    columns = pl.BlockSpec((pixels, wide), lambda g: (0, g))
    rows = hid // 4
    return pl.pallas_call(
        chunk_kernel,
        grid=(8,),
        in_specs=[
            pl.BlockSpec(memory_space=pltpu.SMEM),
            columns,
            columns,
            whole,
            whole,
            pl.BlockSpec((wide, chans), lambda g: (g, 0)),
        ],
        out_specs=[pl.BlockSpec(memory_space=pl.ANY)] * 4,
        out_shape=[pltpu.HBM((rows, chans), BF)] * 4,
        scratch_shapes=[pltpu.VMEM((4, rows, chans), BF), pltpu.SemaphoreType.DMA((4,))],
        compiler_params=pltpu.CompilerParams(vmem_limit_bytes=22 * 1024 * 1024),
        cost_estimate=pl.CostEstimate(
            flops=2 * pixels * hid * chans, bytes_accessed=18 * 1024 * 1024, transcendentals=0
        ),
        name="chunks",
    )(at, d_pre, hidden, normed, d_branch, come)


def on_device(
    image,
    conv_weight,
    conv_bias,
    layernorm_gain,
    layernorm_bias,
    w_expand,
    b_expand,
    w_reduce,
    b_reduce,
    layer_scale,
    cotangent,
):
    rows, cols, chans = image.shape
    hid = w_expand.shape[0]
    per = hid // 256
    scale = 1.0 / math.sqrt(rows * cols * 256)
    first = lax.axis_index("c") == 0
    padded = halo_rows(halo_columns(image, 3), 3)
    kernel = conv_weight.reshape(KS * KS, chans)
    conv_out, normed = conv(
        True,
        padded,
        kernel,
        jnp.stack([conv_bias, layernorm_gain, layernorm_bias] + [layernorm_bias] * 5),
    )
    normed = normed.reshape(rows * cols, chans)
    pre = (
        lax.dot_general(normed, w_expand, (((1,), (1,)), ((), ())), preferred_element_type=F32)
        + b_expand
    )
    act, slope = gelu_pair(pre)
    hidden = act.astype(BF)
    grad_f = cotangent.reshape(rows * cols, chans).astype(F32)
    d_branch = (layer_scale * grad_f).astype(BF)
    d_hidden = jnp.dot(d_branch, w_reduce, preferred_element_type=F32)
    d_pre = (d_hidden * slope).astype(BF)

    far = tdot(jnp.where(first, hidden, d_pre), jnp.where(first, d_branch, normed)).astype(BF)
    come = core_swap(far)
    branch = lax.dot_general(
        hidden, w_reduce, (((1,), (1,)), ((), ())), preferred_element_type=F32
    )
    d_normed = jnp.dot(d_pre, w_expand, preferred_element_type=F32)
    sum_pre = jnp.sum(d_pre.astype(F32), axis=0).reshape(hid // chans, chans)
    params = jnp.stack([layernorm_gain, b_reduce, layer_scale] + [layer_scale] * 5)
    shape = (rows, cols, chans)

    moved = list(chunks(d_pre, hidden, normed, d_branch, come))
    got = split_move(moved, ("x", "y"))
    d_normed, moved[0] = lax.optimization_barrier((d_normed, moved[0]))
    small, d_conv = backward(
        scale,
        padded,
        conv_out,
        d_normed.reshape(shape),
        branch.reshape(shape),
        cotangent,
        sum_pre,
        params,
    )
    total = small.shape[0]
    lower, upper = small[: total // 2], small[total // 2 :]
    small = jnp.where(first, lower, upper) + core_swap(jnp.where(first, upper, lower))
    low = small.astype(BF)
    small = low.astype(F32) + zl_swap(low).astype(F32)
    wide = halo_columns(d_conv, 3)
    d_pad = halo_rows(wide, 3)
    got, small, wide = lax.optimization_barrier((got, small, wide))
    term = add_all([moved[0]] + got).astype(BF).reshape(2, 4, 4, 2 * per, chans)

    moved = split_send(term, small, ("y", "x"), (1, 2))
    got = split_move(moved, ("y", "x"))
    got, d_pad = lax.optimization_barrier((got, d_pad))
    term, small = split_add(moved, got, small.shape[0])
    term = term.astype(BF).reshape(2, 4, 2 * per, chans)

    def image_part(after):
        return conv(False, lax.optimization_barrier((d_pad, after))[0], kernel, cotangent)

    term, small, grad_image = z_sum(term, small, image_part)
    term = term * scale
    top, low = term[:per], term[per:]
    got = core_swap(jnp.concatenate([small, jnp.where(first, low, top)], axis=0))
    keep = jnp.where(first, top, low)
    other, got = got[: total // 2], got[total // 2 :]
    small = jnp.concatenate(
        [jnp.where(first, small, other), jnp.where(first, other, small)], axis=0
    )
    grad_expand = jnp.where(first, keep, got)
    grad_reduce = jnp.where(first, got, keep).T

    kk = KS * KS
    return (
        grad_image,
        grad_expand,
        grad_reduce,
        small[:kk].reshape(KS, KS, chans),
        small[kk],
        small[kk + 1],
        small[kk + 2],
        small[kk + 5 : kk + 5 + hid // chans].reshape(hid),
        small[kk + 3],
        small[kk + 4],
    )


def solution(mesh):
    grid = Mesh(mesh.devices.reshape(SIZES), AXES)
    tile = P(ROW, COL, None)
    one = P()
    in_specs = (tile,) + (one,) * 9 + (tile,)
    out_specs = (tile, P(AXES, None), P(None, AXES)) + (one,) * 7
    return jax.shard_map(
        on_device, mesh=grid, in_specs=in_specs, out_specs=out_specs, check_vma=False
    )
```
